256 devices in a mesh: ctx: 32 (over y, x, z_hi), head: 8 (over z_lo, core).
Axes of the slice: x: 4, y: 4, z: 8 (z_hi: 2, z_lo: 4; z = z_hi * 4 + z_lo), core: 2. Of those that a mesh axis runs over, the one named last changes fastest.
Arguments:
- compressed: bfloat16 [6144, 576], P('ctx'), may hold values from -40 to 40
- query: bfloat16 [6144, 128, 192], P('ctx', 'head'), may hold values from -100 to 100
- d_output: bfloat16 [6144, 128, 128], P('ctx', 'head'), may hold values from -6 to 6
- w_uk: bfloat16 [512, 128, 128], P(None, 'head'), may hold values from -0.25 to 0.25
- w_uv: bfloat16 [512, 128, 128], P(None, 'head'), may hold values from -0.25 to 0.25
Outputs:
- d_query: float32 [6144, 128, 192], P('ctx', 'head')
- d_compressed: float32 [6144, 576], P(('ctx', 'head'))
- d_w_uk: float32 [512, 128, 128], P('ctx', 'head')
- d_w_uv: float32 [512, 128, 128], P('ctx', 'head')
The draws below stay inside these ranges and needn't reach their ends.
All inputs are finite; a program needn't handle non-finite values.
Results may differ from the reference program's by a relative error of at most 0.012.
Values may be sent and summed in bfloat16 or wider, within the bound.
A program may use at most 128 MiB of HBM per device.

```python
import math
import jax
import jax.numpy as jnp
from jax import lax

HEADS = 128
NOPE_DIM = 128
ROPE_DIM = 64
VALUE_DIM = 128
LATENT = 512
TOK_DEV = 192
GROUP = 4
TOKENS = 6144


def shared_draw(key):
    folded = jax.random.fold_in(key, 17)
    subkeys = jax.random.split(folded, 6)
    latent_part = jnp.clip(jax.random.normal(subkeys[1], (TOKENS, LATENT), jnp.float32), -6.0, 6.0)
    rope_part = jnp.clip(jax.random.normal(subkeys[3], (TOKENS, ROPE_DIM), jnp.float32), -6.0, 6.0)
    query_nope = jnp.clip(jax.random.normal(subkeys[4], (TOKENS, HEADS, NOPE_DIM), jnp.float32), -6.0, 6.0)
    query_rope = jnp.clip(jax.random.normal(subkeys[5], (TOKENS, HEADS, ROPE_DIM), jnp.float32), -6.0, 6.0)
    compressed_rows = jnp.concatenate([latent_part, rope_part], axis=1)
    query_rows = jnp.concatenate([query_nope, query_rope], axis=2)
    return (compressed_rows, query_rows)


def draw_compressed(key, part):
    return shared_draw(key)[0].astype(jnp.bfloat16)


def draw_query(key, part):
    return shared_draw(key)[1].astype(jnp.bfloat16)


def levels(rng, shape, shards, smallest, high):
    level = 1.0
    for axis_at, blocks in shards:
        heights = jax.random.uniform(jax.random.fold_in(jax.random.fold_in(rng, 6), axis_at), (blocks,), jnp.float32, smallest / len(shards), high / len(shards))
        level = level * jnp.repeat(jnp.exp(heights), shape[axis_at] // blocks).reshape((-1,) + (1,) * (len(shape) - 1 - axis_at))
    return level


def normal_values(stream_key, dims, scale, most, cuts=(), kind=jnp.bfloat16):
    result = jax.random.normal(stream_key, dims, jnp.float32) * scale
    if len(cuts) > 0:
        result = levels(stream_key, dims, cuts, -0.22, 0.18) * result
    return jnp.clip(result, min=-most, max=most).astype(kind)


def setup_inputs(seed: int = 0) -> dict:
    key_list = jax.random.split(jax.random.key(seed), 6)
    compressed = draw_compressed(jax.random.fold_in(key_list[5], 71), 0)
    query = draw_query(jax.random.fold_in(key_list[5], 71), 0)
    d_output = normal_values(key_list[2], (TOKENS, HEADS, VALUE_DIM), 1.0, 6.0, ((0, 32), (1, 8)))
    w_uk = normal_values(key_list[3], (LATENT, HEADS, NOPE_DIM), LATENT ** -0.5, 0.25, ((1, 8),))
    w_uv = normal_values(key_list[4], (LATENT, HEADS, VALUE_DIM), LATENT ** -0.5, 0.25, ((1, 8),))
    return {"compressed": compressed, "query": query, "d_output": d_output, "w_uk": w_uk, "w_uv": w_uv}


def expand_latent(latent, weight):
    return jnp.einsum('jc,chd->jhd', latent.astype(jnp.float32), weight.astype(jnp.float32)).astype(jnp.bfloat16)

def reference(compressed, query, d_output, w_uk, w_uv):
    span_rows = GROUP * TOK_DEV
    nope_width = w_uk.shape[2]
    score_scale = 1.0 / math.sqrt(query.shape[2])
    uk_wide = w_uk.astype(jnp.float32)
    uv_wide = w_uv.astype(jnp.float32)

    def one_sequence(totals, sequence):
        grad_uk, grad_uv = totals
        first_row = (sequence * span_rows).astype(jnp.int32)
        row_block = lax.dynamic_slice_in_dim(compressed, first_row, span_rows, 0)
        latent = row_block[:, :LATENT]
        key_rope = row_block[:, LATENT:].astype(jnp.float32)
        key_nope = expand_latent(latent, w_uk).astype(jnp.float32)
        values_here = expand_latent(latent, w_uv).astype(jnp.float32)
        key_total = jnp.zeros((span_rows, HEADS, NOPE_DIM), jnp.float32)
        value_total = jnp.zeros((span_rows, HEADS, VALUE_DIM), jnp.float32)
        rope_total = jnp.zeros((span_rows, ROPE_DIM), jnp.float32)
        query_grads = []
        for slab_index in range(GROUP):
            slab_start = (first_row + slab_index * TOK_DEV).astype(jnp.int32)
            query_slab = lax.dynamic_slice_in_dim(query, slab_start, TOK_DEV, 0).astype(jnp.float32)
            output_grad = lax.dynamic_slice_in_dim(d_output, slab_start, TOK_DEV, 0).astype(jnp.float32)
            query_nope = query_slab[..., :nope_width]
            query_rope = query_slab[..., nope_width:]
            scores = (jnp.einsum('ihd,jhd->hij', query_nope, key_nope) + jnp.einsum('ihr,jr->hij', query_rope, key_rope)) * score_scale
            probs = jax.nn.softmax(scores, axis=-1)
            probs_low = probs.astype(jnp.bfloat16).astype(jnp.float32)
            attended = jnp.einsum('hij,jhd->ihd', probs_low, values_here)
            row_delta = lax.optimization_barrier(jnp.sum(output_grad * attended, axis=-1))
            grad_probs = jnp.einsum('ihd,jhd->hij', output_grad, values_here)
            score_grads = probs * (grad_probs - jnp.transpose(row_delta)[:, :, None])
            score_low = score_grads.astype(jnp.bfloat16).astype(jnp.float32)
            grad_nope = jnp.einsum('hij,jhd->ihd', score_low, key_nope)
            grad_rope = jnp.einsum('hij,jr->ihr', score_low, key_rope)
            query_grads.append(jnp.concatenate([grad_nope, grad_rope], axis=-1) * score_scale)
            key_grad = (jnp.einsum('hij,ihd->jhd', score_low, query_nope) * score_scale).astype(jnp.bfloat16)
            value_grad = jnp.einsum('hij,ihd->jhd', probs_low, output_grad).astype(jnp.bfloat16)
            key_total = key_total + key_grad.astype(jnp.float32)
            value_total = value_total + value_grad.astype(jnp.float32)
            rope_total = rope_total + jnp.einsum('hij,ihr->jr', score_low, query_rope) * score_scale
        latent_wide = latent.astype(jnp.float32)
        latent_grad = jnp.einsum('jhd,chd->jc', key_total, uk_wide) + jnp.einsum('jhd,chd->jc', value_total, uv_wide)
        grad_uk = grad_uk + jnp.einsum('jc,jhd->chd', latent_wide, key_total)
        grad_uv = grad_uv + jnp.einsum('jc,jhd->chd', latent_wide, value_total)
        row_grads = jnp.concatenate([latent_grad, rope_total], axis=1)
        return ((grad_uk, grad_uv), (jnp.concatenate(query_grads, axis=0), row_grads))
    start_totals = (jnp.zeros((LATENT, HEADS, NOPE_DIM), jnp.float32), jnp.zeros((LATENT, HEADS, VALUE_DIM), jnp.float32))
    sequences = jnp.arange(TOKENS // span_rows, dtype=jnp.int32)
    final_totals, stacked = lax.scan(one_sequence, start_totals, sequences)
    query_out = stacked[0].reshape(TOKENS, HEADS, NOPE_DIM + ROPE_DIM)
    rows_out = stacked[1].reshape(TOKENS, LATENT + ROPE_DIM)
    return (query_out, rows_out, final_totals[0], final_totals[1])
```

```python
import functools
import math

import jax
import jax.numpy as jnp
from jax import lax
from jax.experimental import pallas as pl
from jax.experimental.pallas import tpu as pltpu
from jax.sharding import Mesh
from jax.sharding import PartitionSpec as P

BF = jnp.bfloat16
F32 = jnp.float32
GROUP = 4
CTX = ("y", "x", "zh")
HEAD = ("zl", "c")
NN = (((1,), (0,)), ((), ()))
NT = (((1,), (1,)), ((), ()))
TN = (((0,), (0,)), ((), ()))


def dot(a, b, dims=NN):
    return lax.dot_general(a, b, dims, preferred_element_type=F32)


def kernel(
    comp_in, query, d_out, w_uk, w_uv,
    dq_o, dc_o, dw_o,
    comp, wraw, qraw, doraw, tmp, wcat, qh, doh, kvg, lat_t, acc, racc, dqs,
    dwb, r1, r2, e1, r3, r4, f1, r5,
    dcs, c1, s1, c2, s2, c3,
    in_sem, dq_sem, gs_sem, gr_sem, ws_sem, wr_sem, cs_sem, cr_sem,
):
    heads, rows, width = qh.shape
    span, latent = acc.shape
    half_rows = rows // 2
    scale = 1.0 / math.sqrt(width)
    to_exp2 = scale * math.log2(math.e)
    chunks = heads // 2

    y, x, zh = lax.axis_index("y"), lax.axis_index("x"), lax.axis_index("zh")
    zl, core = lax.axis_index("zl"), lax.axis_index("c")
    other = 1 - core
    x_lo = x % 2
    x_pair = x + 1 - 2 * x_lo
    slab = x_lo * 2 + zh
    zpos = zh * 4 + zl

    def remote(src, dst, send, recv, where):
        return pltpu.make_async_remote_copy(
            src_ref=src, dst_ref=dst, send_sem=send, recv_sem=recv,
            device_id=where, device_id_type=pl.DeviceIdType.MESH,
        )

    def z_at(pos):
        return {"zh": pos // 4, "zl": pos % 4}

    loads = [
        pltpu.make_async_copy(w_uk, wraw.at[0], in_sem.at[0]),
        pltpu.make_async_copy(w_uv, wraw.at[1], in_sem.at[1]),
        pltpu.make_async_copy(query, qraw, in_sem.at[2]),
        pltpu.make_async_copy(d_out, doraw, in_sem.at[3]),
        pltpu.make_async_copy(
            comp_in, comp.at[pl.ds(pl.multiple_of(slab * rows, 64), rows)], in_sem.at[4]
        ),
    ]
    for load in loads:
        load.start()

    barrier = pltpu.get_barrier_semaphore()
    peers = [
        {"x": (x + 1) % 4}, {"x": (x + 3) % 4}, {"y": (y + 1) % 4}, {"y": (y + 3) % 4}, {"c": other},
    ] + [z_at((zpos + k) % 8) for k in range(1, 8)]
    for peer in peers:
        pl.semaphore_signal(barrier, inc=1, device_id=peer, device_id_type=pl.DeviceIdType.MESH)
    pl.semaphore_wait(barrier, len(peers))

    def part(which, half):
        return comp.at[pl.ds(pl.multiple_of(which * rows + half * half_rows, 32), half_rows)]

    own = comp_in.at[pl.ds(pl.multiple_of(core * half_rows, 32), half_rows)]
    z_slab = x_lo * 2 + 1 - zh
    x_slab = (1 - x_lo) * 2 + zh
    d_slab = (1 - x_lo) * 2 + 1 - zh

    def z_send(k, target):
        return remote(own, part(slab, core), gs_sem.at[k], gr_sem.at[1], {"zh": 1 - zh, "zl": target})

    x_send = remote(own, part(slab, core), gs_sem.at[0], gr_sem.at[0], {"x": x_pair})
    x_send.start()

    @pl.when(zl == 0)
    def _():
        z_send(1, 3).start()
        z_send(2, 2).start()

    @pl.when(zl == 3)
    def _():
        z_send(1, 0).start()
        z_send(2, 1).start()

    def arrived(which, half, k):
        remote(own, part(which, half), gs_sem.at[0], gr_sem.at[k], {"c": other}).wait_recv()

    def swap(which, k):
        return remote(part(which, core), part(which, core), gs_sem.at[k], gr_sem.at[k], {"c": other})

    diag_send = remote(part(z_slab, core), part(z_slab, core), gs_sem.at[3], gr_sem.at[2], {"x": x_pair})
    swaps = [swap(x_slab, 4), swap(z_slab, 5), swap(d_slab, 6)]

    def relayout_weight(t):
        def step(r, carry):
            at = pl.ds(pl.multiple_of(r * 128, 128), 128)
            tmp[pl.ds(0, 128 * heads), :] = wraw[t, at].reshape(128 * heads, 128).astype(F32)
            for h in range(heads):
                wcat[h, at, t * 128 : (t + 1) * 128] = tmp[pl.ds(h, 128, stride=heads), :].astype(BF)
            return carry

        lax.fori_loop(0, latent // 128, step, 0)

    loads[0].wait()
    relayout_weight(0)
    arrived(x_slab, core, 0)
    swaps[0].start()
    arrived(z_slab, core, 1)
    diag_send.start()
    swaps[1].start()
    loads[1].wait()
    relayout_weight(1)
    arrived(d_slab, core, 2)
    swaps[2].start()
    loads[2].wait()
    loads[3].wait()
    nope = 128
    tmp[...] = qraw[:, :, :nope].reshape(rows * heads, nope).astype(F32)
    for h in range(heads):
        qh[h, :, :nope] = tmp[pl.ds(h, rows, stride=heads), :].astype(BF)
    tmp[:, : width - nope] = qraw[:, :, nope:].reshape(rows * heads, width - nope).astype(F32)
    for h in range(heads):
        qh[h, :, nope:] = tmp[pl.ds(h, rows, stride=heads), :][:, : width - nope].astype(BF)
    tmp[...] = doraw[...].reshape(rows * heads, 128).astype(F32)
    for h in range(heads):
        doh[h] = tmp[pl.ds(h, rows, stride=heads), :].astype(BF)
    loads[4].wait()
    arrived(x_slab, other, 4)
    arrived(z_slab, other, 5)
    arrived(d_slab, other, 6)
    x_send.wait_send()
    diag_send.wait_send()
    for s in swaps:
        s.wait_send()

    @pl.when((zl == 0) | (zl == 3))
    def _():
        z_send(1, 0).wait_send()
        z_send(2, 0).wait_send()

    flipped = comp[:, :latent].T
    lat_t[0] = flipped
    for a in range(4):
        for b in range(4):
            lat_t[1, (b * 4 + a) * 32 : (b * 4 + a + 1) * 32] = flipped[(a * 4 + b) * 32 : (a * 4 + b + 1) * 32]
    acc[...] = jnp.zeros_like(acc)
    racc[...] = jnp.zeros_like(racc)

    def head_pass(h, f):
        e = dot(comp[:, :latent], wcat[h]).astype(BF)
        keys = jnp.concatenate([e[:, :128], comp[:, latent:]], axis=1)
        values = e[:, 128:]
        qq, dd = qh[h], doh[h]
        scores = dot(qq, keys, NT)
        top = jnp.max(scores, axis=1, keepdims=True)
        grown = jnp.exp2((scores - top) * to_exp2)
        probs = grown * (1.0 / jnp.sum(grown, axis=1, keepdims=True))
        grad_probs = dot(dd, values, NT)
        probs_low = probs.astype(BF)
        delta = jnp.sum(probs_low.astype(F32) * grad_probs, axis=1, keepdims=True)
        score_low = (probs * (grad_probs - delta)).astype(BF)
        dqs[h] = dot(score_low, keys) * scale
        pltpu.make_async_copy(dqs.at[h], dq_o.at[h], dq_sem.at[h]).start()
        key_grad = dot(score_low, qq, TN) * scale
        kvg[f, :, :128] = key_grad[:, :128].astype(BF)
        racc[...] += key_grad[:, 128:]
        kvg[f, :, 128:] = dot(probs_low, dd, TN).astype(BF)

    first, second = ("y", "x"), ("x", "y")
    at = {"x": x, "y": y}

    def exchange(k, f, n, axis, to_right, to_left, inbox):
        p = at[axis]
        return [
            remote(to_right, inbox.at[k, f, 0], ws_sem.at[k, f, n], wr_sem.at[k, f, n], {axis: (p + 1) % 4}),
            remote(to_left, inbox.at[k, f, 1], ws_sem.at[k, f, n + 1], wr_sem.at[k, f, n + 1], {axis: (p + 3) % 4}),
        ]

    def spread(k, f, n, axis, buf, inbox, size):
        away = (at[axis] + 2) % 4
        b = buf.at[k, f, away]
        return exchange(k, f, n, axis, b.at[pl.ds(0, size)], b.at[pl.ds(size, size)], inbox)

    def pass_on(k, f, n, axis, buf, inbox):
        p = at[axis]
        return exchange(k, f, n, axis, buf.at[k, f, (p + 1) % 4], buf.at[k, f, (p + 3) % 4], inbox)

    def copies(k, f, stage):
        if stage == 0:
            return spread(k, f, 0, first[f], dwb, r1, 64)
        if stage == 1:
            return pass_on(k, f, 2, first[f], dwb, r2)
        if stage == 2:
            return spread(k, f, 4, second[f], e1, r3, 16)
        if stage == 3:
            return pass_on(k, f, 6, second[f], e1, r4)
        return [remote(f1.at[k, f, 1 - zh], r5.at[k, f], ws_sem.at[k, f, 8], wr_sem.at[k, f, 8], {"zh": 1 - zh})]

    def fold(k, f, axis, buf, inbox, size):
        p = at[axis]
        right, left = (p + 1) % 4, (p + 3) % 4
        buf[k, f, right, :size] = (buf[k, f, right, :size].astype(F32) + inbox[k, f, 0].astype(F32)).astype(BF)
        buf[k, f, left, size:] = (buf[k, f, left, size:].astype(F32) + inbox[k, f, 1].astype(F32)).astype(BF)

    def total(k, f, axis, buf, inbox):
        return buf[k, f, at[axis]].astype(F32) + inbox[k, f, 0].astype(F32) + inbox[k, f, 1].astype(F32)

    def advance(stage, k):
        for f in range(2):
            for c in copies(k, f, stage - 1):
                c.wait_recv()
            if stage == 1:
                fold(k, f, first[f], dwb, r1, 64)
            elif stage == 2:
                e1[k, f] = total(k, f, first[f], dwb, r2).astype(BF).reshape(4, 32, 256)
            elif stage == 3:
                fold(k, f, second[f], e1, r3, 16)
            elif stage == 4:
                f1[k, f] = total(k, f, second[f], e1, r4).astype(BF).reshape(2, 16, 256)
            else:
                dw_o[2 * k + f] = f1[k, f, zh].astype(F32) + r5[k, f].astype(F32)
            if stage < 5:
                for c in copies(k, f, stage):
                    c.start()

    def chunk_step(t, carry):
        for f in range(2):
            head_pass(2 * t + f, f)
        both = dot(kvg[0], wcat[2 * t], NT) + dot(kvg[1], wcat[2 * t + 1], NT)
        acc[...] += both
        for f in range(2):
            dwb[t, f] = dot(lat_t[f], kvg[f]).astype(BF).reshape(4, 128, 256)
        for stage in range(5, 0, -1):
            @pl.when(t >= stage)
            def _():
                advance(stage, t - stage)
        for f in range(2):
            for c in copies(t, f, 0):
                c.start()
        return carry

    lax.fori_loop(0, chunks, chunk_step, 0)

    for b in range(GROUP):
        for s in range(8):
            r0 = (b * 8 + s) * 24
            dcs[s % 2, b // 2, b % 2, s // 2, :, :latent] = acc[r0 : r0 + 24].astype(BF)
            dcs[s % 2, b // 2, b % 2, s // 2, :, latent:] = (racc[r0 : r0 + 24]).astype(BF)
    send1 = remote(dcs.at[other], c1, cs_sem.at[0], cr_sem.at[0], {"c": other})
    send1.start()
    send2 = remote(s1.at[1 - x_lo], c2, cs_sem.at[1], cr_sem.at[1], {"x": x_pair})
    sends3 = [
        remote(s2.at[(zpos + k) % 8], c3.at[k - 1], cs_sem.at[1 + k], cr_sem.at[1 + k], z_at((zpos + k) % 8))
        for k in range(1, 8)
    ]

    def tail(t):
        for stage in range(5, 0, -1):
            if 0 <= t - stage < chunks:
                advance(stage, t - stage)

    send1.wait_recv()
    s1[...] = (dcs[core].astype(F32) + c1[...].astype(F32)).astype(BF)
    send2.start()
    tail(chunks)
    send2.wait_recv()
    s2[...] = (s1[x_lo].astype(F32) + c2[...].astype(F32)).astype(BF).reshape(s2.shape)
    for s in sends3:
        s.start()
    tail(chunks + 1)
    tail(chunks + 2)
    sum3 = s2[zpos].astype(F32)
    for k, s in enumerate(sends3):
        s.wait_recv()
        sum3 += c3[k].astype(F32)
    dc_o[...] = sum3
    tail(chunks + 3)
    tail(chunks + 4)

    send1.wait_send()
    send2.wait_send()
    for s in sends3:
        s.wait_send()

    def drain(k, carry):
        for f in range(2):
            for stage in range(5):
                for c in copies(k, f, stage):
                    c.wait_send()
            h = 2 * k + f
            pltpu.make_async_copy(dqs.at[h], dq_o.at[h], dq_sem.at[h]).wait()
        return carry

    lax.fori_loop(0, chunks, drain, 0)


def per_device(compressed, query, d_output, w_uk, w_uv):
    rows, columns = compressed.shape
    latent, heads, nope = w_uk.shape
    width = query.shape[2]
    span = GROUP * rows
    chunks = heads // 2
    anywhere = pl.BlockSpec(memory_space=pl.ANY)
    vmem = pl.BlockSpec(memory_space=pltpu.VMEM)
    dma = pltpu.SemaphoreType.DMA
    dq, dc, dw = pl.pallas_call(
        kernel,
        out_shape=[
            jax.ShapeDtypeStruct((heads, rows, width), F32),
            jax.ShapeDtypeStruct((24, columns), F32),
            jax.ShapeDtypeStruct((heads, 16, 256), F32),
        ],
        in_specs=[anywhere] * 5,
        out_specs=[anywhere, vmem, vmem],
        scratch_shapes=[
            pltpu.VMEM((span, columns), BF),
            pltpu.VMEM((2, latent, heads, 128), BF),
            pltpu.VMEM((rows, heads, width), BF),
            pltpu.VMEM((rows, heads, 128), BF),
            pltpu.VMEM((rows * heads, 128), F32),
            pltpu.VMEM((heads, latent, 256), BF),
            pltpu.VMEM((heads, rows, width), BF),
            pltpu.VMEM((heads, rows, 128), BF),
            pltpu.VMEM((2, span, 256), BF),
            pltpu.VMEM((2, latent, span), BF),
            pltpu.VMEM((span, latent), F32),
            pltpu.VMEM((span, width - nope), F32),
            pltpu.VMEM((heads, rows, width), F32),
            pltpu.VMEM((chunks, 2, 4, 128, 256), BF),
            pltpu.VMEM((chunks, 2, 2, 64, 256), BF),
            pltpu.VMEM((chunks, 2, 2, 128, 256), BF),
            pltpu.VMEM((chunks, 2, 4, 32, 256), BF),
            pltpu.VMEM((chunks, 2, 2, 16, 256), BF),
            pltpu.VMEM((chunks, 2, 2, 32, 256), BF),
            pltpu.VMEM((chunks, 2, 2, 16, 256), BF),
            pltpu.VMEM((chunks, 2, 16, 256), BF),
            pltpu.VMEM((2, 2, 2, 4, 24, columns), BF),
            pltpu.VMEM((2, 2, 4, 24, columns), BF),
            pltpu.VMEM((2, 2, 4, 24, columns), BF),
            pltpu.VMEM((2, 4, 24, columns), BF),
            pltpu.VMEM((8, 24, columns), BF),
            pltpu.VMEM((7, 24, columns), BF),
            dma((5,)), dma((heads,)), dma((7,)), dma((7,)),
            dma((chunks, 2, 9)), dma((chunks, 2, 9)), dma((9,)), dma((9,)),
        ],
        compiler_params=pltpu.CompilerParams(
            collective_id=0, has_side_effects=True, vmem_limit_bytes=58 * 2**20
        ),
        cost_estimate=pl.CostEstimate(
            flops=14_000_000_000, bytes_accessed=10_000_000, transcendentals=2_400_000
        ),
    )(compressed, query, d_output, w_uk, w_uv)
    d_query = jnp.transpose(dq, (1, 0, 2))
    dw = jnp.transpose(dw, (1, 0, 2))
    return d_query, dc, dw[:, :, :128], dw[:, :, 128:]


def solution(mesh):
    torus = Mesh(mesh.devices.reshape(4, 4, 2, 4, 2), CTX + HEAD)
    return jax.shard_map(
        per_device,
        mesh=torus,
        in_specs=(
            P(CTX, None),
            P(CTX, HEAD, None),
            P(CTX, HEAD, None),
            P(None, HEAD, None),
            P(None, HEAD, None),
        ),
        out_specs=(
            P(CTX, HEAD, None),
            P(CTX + HEAD, None),
            P(CTX, HEAD, None),
            P(CTX, HEAD, None),
        ),
        check_vma=False,
    )
```

```python
import functools
import math

import jax
import jax.numpy as jnp
from jax import lax
from jax.experimental import pallas as pl
from jax.experimental.pallas import tpu as pltpu
from jax.sharding import Mesh
from jax.sharding import PartitionSpec as P

BF = jnp.bfloat16
F32 = jnp.float32
GROUP = 4
LAG = (0, 2, 4, 6, 8)
DIRECT = 2
CTX = ("y", "x", "zh")
HEAD = ("zl", "c")
NN = (((1,), (0,)), ((), ()))
NT = (((1,), (1,)), ((), ()))
TN = (((0,), (0,)), ((), ()))


def dot(a, b, dims=NN):
    return lax.dot_general(a, b, dims, preferred_element_type=F32)


def kernel(
    comp_in, query, d_out, w_uk, w_uv,
    dq_o, dc_o, dw_o,
    comp, wraw, qraw, doraw, tmp, wcat, qh, doh, kv, kvg, lat_t, acc, racc, dqs,
    dwb, r1, r2, e1, r3, f1, r4,
    dcs, c1, s1, c2, s2, c3,
    in_sem, gs_sem, gr_sem, ws_sem, wr_sem, cs_sem, cr_sem,
):
    heads, rows, width = qh.shape
    span, latent = acc.shape
    half_rows = rows // 2
    scale = 1.0 / math.sqrt(width)
    to_exp2 = scale * math.log2(math.e)
    chunks = heads // 2

    y, x, zh = lax.axis_index("y"), lax.axis_index("x"), lax.axis_index("zh")
    zl, core = lax.axis_index("zl"), lax.axis_index("c")
    other = 1 - core
    x_lo = x % 2
    x_pair = x + 1 - 2 * x_lo
    slab = x_lo * 2 + zh
    zpos = zh * 4 + zl

    def turn(p, k):
        return (p + k) % 4

    x_other, core_other, zh_other = {"x": x_pair}, {"c": other}, {"zh": 1 - zh}
    z_pos = [(zpos + k) % 8 for k in range(1, 8)]
    z_ring = [{"zh": q // 4, "zl": q % 4} for q in z_pos]

    def remote(src, dst, send, recv, where):
        return pltpu.make_async_remote_copy(
            src_ref=src, dst_ref=dst, send_sem=send, recv_sem=recv,
            device_id=where, device_id_type=pl.DeviceIdType.MESH,
        )

    loads = [
        pltpu.make_async_copy(w_uk, wraw.at[0], in_sem.at[0]),
        pltpu.make_async_copy(w_uv, wraw.at[1], in_sem.at[1]),
        pltpu.make_async_copy(query, qraw, in_sem.at[2]),
        pltpu.make_async_copy(d_out, doraw, in_sem.at[3]),
        pltpu.make_async_copy(
            comp_in, comp.at[pl.ds(pl.multiple_of(slab * rows, 64), rows)], in_sem.at[4]
        ),
    ]
    for load in loads:
        load.start()

    barrier = pltpu.get_barrier_semaphore()
    peers = [{axis: turn(p, k)} for axis, p in (("x", x), ("y", y)) for k in (1, 2, 3)] + [core_other] + z_ring
    for peer in peers:
        pl.semaphore_signal(barrier, inc=1, device_id=peer, device_id_type=pl.DeviceIdType.MESH)

    def relayout_weight(t):
        def step(r, carry):
            at = pl.ds(pl.multiple_of(r * 128, 128), 128)
            tmp[pl.ds(0, 128 * heads), :] = wraw[t, at].reshape(128 * heads, 128).astype(F32)
            for h in range(heads):
                wcat[h, at, t * 128 : (t + 1) * 128] = tmp[pl.ds(h, 128, stride=heads), :].astype(BF)
            return carry

        lax.fori_loop(0, latent // 128, step, 0)

    loads[0].wait()
    relayout_weight(0)
    pl.semaphore_wait(barrier, len(peers))

    def part(which, half):
        return comp.at[pl.ds(pl.multiple_of(which * rows + half * half_rows, 32), half_rows)]

    own = comp_in.at[pl.ds(pl.multiple_of(core * half_rows, 32), half_rows)]
    z_slab = x_lo * 2 + 1 - zh
    x_slab = (1 - x_lo) * 2 + zh
    d_slab = (1 - x_lo) * 2 + 1 - zh

    def z_send(k, target):
        return remote(own, part(slab, core), gs_sem.at[k], gr_sem.at[1], {"zh": 1 - zh, "zl": target})

    x_send = remote(own, part(slab, core), gs_sem.at[0], gr_sem.at[0], x_other)
    x_send.start()

    @pl.when(zl == 0)
    def _():
        z_send(1, 3).start()
        z_send(2, 2).start()

    @pl.when(zl == 3)
    def _():
        z_send(1, 0).start()
        z_send(2, 1).start()

    def arrived(which, half, k):
        remote(own, part(which, half), gs_sem.at[0], gr_sem.at[k], core_other).wait_recv()

    def swap(which, k):
        return remote(part(which, core), part(which, core), gs_sem.at[k], gr_sem.at[k], core_other)

    diag_send = remote(part(z_slab, core), part(z_slab, core), gs_sem.at[3], gr_sem.at[2], x_other)
    swaps = [swap(x_slab, 4), swap(z_slab, 5), swap(d_slab, 6)]

    def expand(which):
        at = pl.ds(pl.multiple_of(which * rows, 64), rows)
        piece = comp[at, :latent]

        def step(h, carry):
            kv[2 * h, at] = dot(piece, wcat[2 * h]).astype(BF)
            kv[2 * h + 1, at] = dot(piece, wcat[2 * h + 1]).astype(BF)
            return carry

        lax.fori_loop(0, heads // 2, step, 0)

    loads[1].wait()
    relayout_weight(1)
    arrived(x_slab, core, 0)
    swaps[0].start()
    loads[2].wait()
    loads[3].wait()
    nope = 128
    tmp[: rows * heads] = qraw[:, :, :nope].reshape(rows * heads, nope).astype(F32)
    for h in range(heads):
        qh[h, :, :nope] = tmp[pl.ds(h, rows, stride=heads), :].astype(BF)
    tmp[: rows * heads, : width - nope] = qraw[:, :, nope:].reshape(rows * heads, width - nope).astype(F32)
    for h in range(heads):
        qh[h, :, nope:] = tmp[pl.ds(h, rows, stride=heads), :][:, : width - nope].astype(BF)
    tmp[: rows * heads] = doraw[...].reshape(rows * heads, 128).astype(F32)
    for h in range(heads):
        doh[h] = tmp[pl.ds(h, rows, stride=heads), :].astype(BF)
    arrived(z_slab, core, 1)
    diag_send.start()
    swaps[1].start()
    loads[4].wait()
    expand(slab)
    arrived(x_slab, other, 4)
    expand(x_slab)
    arrived(d_slab, core, 2)
    swaps[2].start()
    arrived(z_slab, other, 5)
    expand(z_slab)
    acc[...] = jnp.zeros_like(acc)
    racc[...] = jnp.zeros_like(racc)
    arrived(d_slab, other, 6)
    expand(d_slab)
    x_send.wait_send()
    diag_send.wait_send()
    for s in swaps:
        s.wait_send()

    @pl.when((zl == 0) | (zl == 3))
    def _():
        z_send(1, 0).wait_send()
        z_send(2, 0).wait_send()

    flipped = comp[:, :latent].T
    lat_t[0] = flipped
    for a in range(4):
        for b in range(4):
            lat_t[1, (b * 4 + a) * 32 : (b * 4 + a + 1) * 32] = flipped[(a * 4 + b) * 32 : (a * 4 + b + 1) * 32]

    def weigh(h):
        keys = jnp.concatenate([kv[h, :, :128], comp[:, latent:]], axis=1)
        qq, dd = qh[h], doh[h]
        scores = dot(qq, keys, NT)
        grad_probs = dot(dd, kv[h, :, 128:], NT)
        top = jnp.max(scores, axis=1, keepdims=True)
        grown = jnp.exp2((scores - top) * to_exp2)
        probs = grown * (1.0 / jnp.sum(grown, axis=1, keepdims=True))
        probs_low = probs.astype(BF)
        delta = jnp.sum(probs_low.astype(F32) * grad_probs, axis=1, keepdims=True)
        score_low = (probs * (grad_probs - delta)).astype(BF)
        return keys, qq, dd, probs_low, score_low

    def grads(h, f, keys, qq, dd, probs_low, score_low):
        dqs[h] = dot(score_low, keys) * scale
        key_grad = dot(score_low, qq, TN) * scale
        kvg[f, :, :128] = key_grad[:, :128].astype(BF)
        racc[...] += key_grad[:, 128:]
        kvg[f, :, 128:] = dot(probs_low, dd, TN).astype(BF)

    ways = (
        (y, "y", turn(y, 1), turn(y, 3), turn(y, 2)),
        (x, "x", turn(x, 1), turn(x, 3), turn(x, 2)),
    )
    straight = chunks - DIRECT

    def send(k, f, n, src, inbox, where):
        return remote(src, inbox, ws_sem.at[k, f, n], wr_sem.at[k, f, n], where)

    def copies(k, f, stage):
        p, axis, right, left, away = ways[f if stage < 2 else 1 - f]
        right_id, left_id, far_id = {axis: right}, {axis: left}, {axis: away}
        if stage == 0:
            b = dwb.at[k, f, away]
            skip = k // straight
            return [
                send(k, f, 0, b.at[pl.ds(0, 64)], r1.at[k, f, 0], {axis: (p + 1 + skip) % 4}),
                send(k, f, 1, b.at[pl.ds(64, 64)], r1.at[k, f, 1], {axis: (p + 3 - skip) % 4}),
            ]
        if stage == 1:
            return [
                send(k, f, 2, dwb.at[k, f, right], r2.at[k, f, 0], right_id),
                send(k, f, 3, dwb.at[k, f, left], r2.at[k, f, 1], left_id),
            ]
        if stage == 2:
            return [
                send(k, f, 4, e1.at[k, f, away], r3.at[k, f, 2], far_id),
                send(k, f, 5, e1.at[k, f, right], r3.at[k, f, 0], right_id),
                send(k, f, 6, e1.at[k, f, left], r3.at[k, f, 1], left_id),
            ]
        return [send(k, f, 7, f1.at[k, f, 1 - zh], r4.at[k, f], zh_other)]

    def advance(stage, k):
        last = isinstance(k, int) and k >= straight
        for f in range(2):
            for c in copies(k, f, stage - 1):
                c.wait_recv()
            p, _, right, left, _ = ways[f if stage < 3 else 1 - f]
            if stage == 1:
                dwb[k, f, right, :64] = (dwb[k, f, right, :64].astype(F32) + r1[k, f, 0].astype(F32)).astype(BF)
                dwb[k, f, left, 64:] = (dwb[k, f, left, 64:].astype(F32) + r1[k, f, 1].astype(F32)).astype(BF)
            elif stage == 2:
                total = dwb[k, f, p].astype(F32) + r2[k, f, 0].astype(F32) + r2[k, f, 1].astype(F32)
                if last:
                    for c in copies(k, f, 0):
                        c.wait_recv()
                    total += r1[k, f].reshape(128, 256).astype(F32)
                e1[k, f] = total.astype(BF).reshape(4, 32, 256)
            elif stage == 3:
                total = e1[k, f, p].astype(F32)
                for q in range(3):
                    total += r3[k, f, q].astype(F32)
                f1[k, f] = total.astype(BF).reshape(2, 16, 256)
            else:
                dw_o[2 * k + f] = f1[k, f, zh].astype(F32) + r4[k, f].astype(F32)
            if stage < 4:
                for c in copies(k, f, stage):
                    c.start()

    send1 = remote(dcs.at[other], c1, cs_sem.at[0], cr_sem.at[0], core_other)

    def pack_latent():
        for b in range(GROUP):
            for s in range(8):
                r0 = (b * 8 + s) * 24
                dcs[s % 2, (b % 2) * 4 + s // 2, b // 2, :, :latent] = acc[r0 : r0 + 24].astype(BF)
                dcs[s % 2, (b % 2) * 4 + s // 2, b // 2, :, latent:] = racc[r0 : r0 + 24].astype(BF)
        send1.start()

    def chunk_step(t, carry):
        weighed = [weigh(2 * t + f) for f in range(2)]
        for f in range(2):
            grads(2 * t + f, f, *weighed[f])
        both = dot(kvg[0], wcat[2 * t], NT) + dot(kvg[1], wcat[2 * t + 1], NT)
        acc[...] += both
        pl.when(t == chunks - 1)(pack_latent)
        for f in range(2):
            dwb[t, f] = dot(lat_t[f], kvg[f]).astype(BF).reshape(4, 128, 256)
        for f in range(2):
            for c in copies(t, f, 0):
                c.start()

        @pl.when(t >= straight)
        def _():
            for f in range(2):
                for c in copies(t, f, 1):
                    c.start()

        for stage in [q for q in range(1, 5) if LAG[q] < chunks]:
            @pl.when(t >= LAG[stage])
            def _():
                advance(stage, t - LAG[stage])
        return carry

    lax.fori_loop(0, chunks, chunk_step, 0)

    sends2 = [
        remote(s1.at[z_pos[k]], c2.at[k], cs_sem.at[2 + k], cr_sem.at[2 + k], z_ring[k]) for k in range(7)
    ]
    send3 = remote(s2.at[1 - x_lo], c3, cs_sem.at[1], cr_sem.at[1], x_other)

    def tail(t):
        for stage in range(1, 5):
            k = t - LAG[stage]
            if 0 <= k < (straight if stage == 1 else chunks):
                advance(stage, k)

    out_copies = [pltpu.make_async_copy(dqs, dq_o, in_sem.at[0])]
    for c in out_copies:
        c.start()
    send1.wait_recv()
    s1[...] = (dcs[core].astype(F32) + c1[...].astype(F32)).astype(BF)
    for s in sends2:
        s.start()
    for t in range(chunks, chunks + LAG[3]):
        tail(t)
    across = s1[zpos].astype(F32)
    for k, s in enumerate(sends2):
        s.wait_recv()
        across += c2[k].astype(F32)
    s2[...] = across.astype(BF)
    send3.start()
    for t in range(chunks + LAG[3], chunks + LAG[4]):
        tail(t)
    send3.wait_recv()
    dc_o[...] = s2[x_lo].astype(F32) + c3[...].astype(F32)

    for c in out_copies:
        c.wait()
    send1.wait_send()
    send3.wait_send()
    for s in sends2:
        s.wait_send()

    def drain(k, carry):
        for f in range(2):
            for stage in range(4):
                for c in copies(k, f, stage):
                    c.wait_send()
        return carry

    lax.fori_loop(0, chunks, drain, 0)


def per_device(compressed, query, d_output, w_uk, w_uv):
    rows, columns = compressed.shape
    latent, heads, nope = w_uk.shape
    width = query.shape[2]
    span = GROUP * rows
    chunks = heads // 2
    anywhere = pl.BlockSpec(memory_space=pl.ANY)
    vmem = pl.BlockSpec(memory_space=pltpu.VMEM)
    dma = pltpu.SemaphoreType.DMA
    dq, dc, dw = pl.pallas_call(
        kernel,
        out_shape=[
            jax.ShapeDtypeStruct((heads, rows, width), F32),
            jax.ShapeDtypeStruct((24, columns), F32),
            jax.ShapeDtypeStruct((heads, 16, 256), F32),
        ],
        in_specs=[pl.BlockSpec(memory_space=pltpu.HBM)] * 5,
        out_specs=[anywhere, vmem, vmem],
        scratch_shapes=[
            pltpu.VMEM((span, columns), BF),
            pltpu.VMEM((2, latent, heads, 128), BF),
            pltpu.VMEM((rows, heads, width), BF),
            pltpu.VMEM((rows, heads, 128), BF),
            pltpu.VMEM((rows * heads + heads, 128), F32),
            pltpu.VMEM((heads, latent, 256), BF),
            pltpu.VMEM((heads, rows, width), BF),
            pltpu.VMEM((heads, rows, 128), BF),
            pltpu.VMEM((heads, span, 256), BF),
            pltpu.VMEM((2, span, 256), BF),
            pltpu.VMEM((2, latent, span), BF),
            pltpu.VMEM((span, latent), F32),
            pltpu.VMEM((span, width - nope), F32),
            pltpu.VMEM((heads, rows, width), F32),
            pltpu.VMEM((chunks, 2, 4, 128, 256), BF),
            pltpu.VMEM((chunks, 2, 2, 64, 256), BF),
            pltpu.VMEM((chunks, 2, 2, 128, 256), BF),
            pltpu.VMEM((chunks, 2, 4, 32, 256), BF),
            pltpu.VMEM((chunks, 2, 3, 32, 256), BF),
            pltpu.VMEM((chunks, 2, 2, 16, 256), BF),
            pltpu.VMEM((chunks, 2, 16, 256), BF),
            pltpu.VMEM((2, 8, 2, 24, columns), BF),
            pltpu.VMEM((8, 2, 24, columns), BF),
            pltpu.VMEM((8, 2, 24, columns), BF),
            pltpu.VMEM((7, 2, 24, columns), BF),
            pltpu.VMEM((2, 24, columns), BF),
            pltpu.VMEM((24, columns), BF),
            dma((5,)), dma((7,)), dma((7,)),
            dma((chunks, 2, 8)), dma((chunks, 2, 8)), dma((9,)), dma((9,)),
        ],
        compiler_params=pltpu.CompilerParams(
            collective_id=0, has_side_effects=True, vmem_limit_bytes=57 * 2**20
        ),
        cost_estimate=pl.CostEstimate(
            flops=14_000_000_000, bytes_accessed=10_000_000, transcendentals=2_400_000
        ),
    )(compressed, query, d_output, w_uk, w_uv)
    dq = jnp.transpose(dq, (1, 0, 2))
    dw = jnp.transpose(dw, (1, 0, 2))
    return dq, dc, dw[:, :, :128], dw[:, :, 128:]


def solution(mesh):
    torus = Mesh(mesh.devices.reshape(4, 4, 2, 4, 2), CTX + HEAD)
    return jax.shard_map(
        per_device,
        mesh=torus,
        in_specs=(
            P(CTX, None),
            P(CTX, HEAD, None),
            P(CTX, HEAD, None),
            P(None, HEAD, None),
            P(None, HEAD, None),
        ),
        out_specs=(
            P(CTX, HEAD, None),
            P(CTX + HEAD, None),
            P(CTX, HEAD, None),
            P(CTX, HEAD, None),
        ),
        check_vma=False,
    )
```

```python
import functools
import math

import jax
import jax.numpy as jnp
from jax import lax
from jax.experimental import pallas as pl
from jax.experimental.pallas import tpu as pltpu
from jax.sharding import Mesh
from jax.sharding import PartitionSpec as P

BF = jnp.bfloat16
F32 = jnp.float32
GROUP = 4
LAG = (0, 2, 4, 6, 8)
DIRECT = 2
CTX = ("y", "x", "zh")
HEAD = ("zl", "c")
NN = (((1,), (0,)), ((), ()))
NT = (((1,), (1,)), ((), ()))
TN = (((0,), (0,)), ((), ()))


def dot(a, b, dims=NN):
    return lax.dot_general(a, b, dims, preferred_element_type=F32)


def kernel(
    comp_in, query, d_out, w_uk, w_uv,
    dq_o, dc_o, dw_o,
    comp, wraw, qraw, doraw, tmp, wcat, qh, doh, kv, kvg, lat_t, acc, racc, dqn, dqr,
    dwb, r1, r2, e1, r3, f1, r4,
    dcs, c1, s1, c2, s2, c3,
    in_sem, gs_sem, gr_sem, ws_sem, wr_sem, cs_sem, cr_sem,
):
    heads, rows, width = qh.shape
    span, latent = acc.shape
    half_rows = rows // 2
    scale = 1.0 / math.sqrt(width)
    to_exp2 = scale * math.log2(math.e)
    chunks = heads // 2

    y, x, zh = lax.axis_index("y"), lax.axis_index("x"), lax.axis_index("zh")
    zl, core = lax.axis_index("zl"), lax.axis_index("c")
    other = 1 - core
    x_lo = x % 2
    x_pair = x + 1 - 2 * x_lo
    slab = x_lo * 2 + zh
    zpos = zh * 4 + zl

    def turn(p, k):
        return (p + k) % 4

    x_other, core_other, zh_other = {"x": x_pair}, {"c": other}, {"zh": 1 - zh}
    z_pos = [(zpos + k) % 8 for k in range(1, 8)]
    z_ring = [{"zh": q // 4, "zl": q % 4} for q in z_pos]

    def remote(src, dst, send, recv, where):
        return pltpu.make_async_remote_copy(
            src_ref=src, dst_ref=dst, send_sem=send, recv_sem=recv,
            device_id=where, device_id_type=pl.DeviceIdType.MESH,
        )

    loads = [
        pltpu.make_async_copy(w_uk, wraw.at[0], in_sem.at[0]),
        pltpu.make_async_copy(w_uv, wraw.at[1], in_sem.at[1]),
        pltpu.make_async_copy(query, qraw, in_sem.at[2]),
        pltpu.make_async_copy(d_out, doraw, in_sem.at[3]),
        pltpu.make_async_copy(
            comp_in, comp.at[pl.ds(pl.multiple_of(slab * rows, 64), rows)], in_sem.at[4]
        ),
    ]
    for load in loads:
        load.start()

    barrier = pltpu.get_barrier_semaphore()
    peers = [{axis: turn(p, k)} for axis, p in (("x", x), ("y", y)) for k in (1, 2, 3)] + [core_other] + z_ring
    for peer in peers:
        pl.semaphore_signal(barrier, inc=1, device_id=peer, device_id_type=pl.DeviceIdType.MESH)

    def relayout_weight(t):
        def step(r, carry):
            at = pl.ds(pl.multiple_of(r * 128, 128), 128)
            tmp[pl.ds(0, 128 * heads), :] = wraw[t, at].reshape(128 * heads, 128).astype(F32)
            for h in range(heads):
                wcat[h, at, t * 128 : (t + 1) * 128] = tmp[pl.ds(h, 128, stride=heads), :].astype(BF)
            return carry

        lax.fori_loop(0, latent // 128, step, 0)

    loads[0].wait()
    relayout_weight(0)
    pl.semaphore_wait(barrier, len(peers))

    def part(which, half):
        return comp.at[pl.ds(pl.multiple_of(which * rows + half * half_rows, 32), half_rows)]

    own = comp_in.at[pl.ds(pl.multiple_of(core * half_rows, 32), half_rows)]
    z_slab = x_lo * 2 + 1 - zh
    x_slab = (1 - x_lo) * 2 + zh
    d_slab = (1 - x_lo) * 2 + 1 - zh

    def z_send(k, target):
        return remote(own, part(slab, core), gs_sem.at[k], gr_sem.at[1], {"zh": 1 - zh, "zl": target})

    x_send = remote(own, part(slab, core), gs_sem.at[0], gr_sem.at[0], x_other)
    x_send.start()

    @pl.when(zl == 0)
    def _():
        z_send(1, 3).start()
        z_send(2, 2).start()

    @pl.when(zl == 3)
    def _():
        z_send(1, 0).start()
        z_send(2, 1).start()

    def arrived(which, half, k):
        remote(own, part(which, half), gs_sem.at[0], gr_sem.at[k], core_other).wait_recv()

    def swap(which, k):
        return remote(part(which, core), part(which, core), gs_sem.at[k], gr_sem.at[k], core_other)

    diag_send = remote(part(z_slab, core), part(z_slab, core), gs_sem.at[3], gr_sem.at[2], x_other)
    swaps = [swap(x_slab, 4), swap(z_slab, 5), swap(d_slab, 6)]

    def expand(which):
        at = pl.ds(pl.multiple_of(which * rows, 64), rows)
        piece = comp[at, :latent]

        def step(h, carry):
            kv[2 * h, at] = dot(piece, wcat[2 * h]).astype(BF)
            kv[2 * h + 1, at] = dot(piece, wcat[2 * h + 1]).astype(BF)
            return carry

        lax.fori_loop(0, heads // 2, step, 0)

    loads[1].wait()
    relayout_weight(1)
    arrived(x_slab, core, 0)
    swaps[0].start()
    loads[2].wait()
    loads[3].wait()
    nope = 128
    tmp[: rows * heads] = qraw[:, :, :nope].reshape(rows * heads, nope).astype(F32)
    for h in range(heads):
        qh[h, :, :nope] = tmp[pl.ds(h, rows, stride=heads), :].astype(BF)
    tmp[: rows * heads, : width - nope] = qraw[:, :, nope:].reshape(rows * heads, width - nope).astype(F32)
    for h in range(heads):
        qh[h, :, nope:] = tmp[pl.ds(h, rows, stride=heads), :][:, : width - nope].astype(BF)
    tmp[: rows * heads] = doraw[...].reshape(rows * heads, 128).astype(F32)
    for h in range(heads):
        doh[h] = tmp[pl.ds(h, rows, stride=heads), :].astype(BF)
    arrived(z_slab, core, 1)
    diag_send.start()
    swaps[1].start()
    loads[4].wait()
    expand(slab)
    arrived(x_slab, other, 4)
    expand(x_slab)
    arrived(d_slab, core, 2)
    swaps[2].start()
    arrived(z_slab, other, 5)
    expand(z_slab)
    acc[...] = jnp.zeros_like(acc)
    racc[...] = jnp.zeros_like(racc)
    arrived(d_slab, other, 6)
    expand(d_slab)
    x_send.wait_send()
    diag_send.wait_send()
    for s in swaps:
        s.wait_send()

    @pl.when((zl == 0) | (zl == 3))
    def _():
        z_send(1, 0).wait_send()
        z_send(2, 0).wait_send()

    flipped = comp[:, :latent].T
    lat_t[0] = flipped
    for a in range(4):
        for b in range(4):
            lat_t[1, (b * 4 + a) * 32 : (b * 4 + a + 1) * 32] = flipped[(a * 4 + b) * 32 : (a * 4 + b + 1) * 32]

    def weigh(h):
        keys = jnp.concatenate([kv[h, :, :128], comp[:, latent:]], axis=1)
        qq, dd = qh[h], doh[h]
        scores = dot(qq, keys, NT)
        grad_probs = dot(dd, kv[h, :, 128:], NT)
        top = jnp.max(scores, axis=1, keepdims=True)
        grown = jnp.exp2((scores - top) * to_exp2)
        probs = grown * (1.0 / jnp.sum(grown, axis=1, keepdims=True))
        probs_low = probs.astype(BF)
        delta = jnp.sum(probs_low.astype(F32) * grad_probs, axis=1, keepdims=True)
        score_low = (probs * (grad_probs - delta)).astype(BF)
        return keys, qq, dd, probs_low, score_low

    def grads(h, f, keys, qq, dd, probs_low, score_low):
        d_q = dot(score_low, keys) * scale
        dqn[pl.ds(h, rows, stride=heads), :] = d_q[:, :128]
        dqr[pl.ds(h, rows, stride=heads), :] = jnp.concatenate(
            [d_q[:, 128:], jnp.zeros((rows, 256 - width), F32)], axis=1
        )
        key_grad = dot(score_low, qq, TN) * scale
        kvg[f, :, :128] = key_grad[:, :128].astype(BF)
        racc[...] += key_grad[:, 128:]
        kvg[f, :, 128:] = dot(probs_low, dd, TN).astype(BF)

    ways = (
        (y, "y", turn(y, 1), turn(y, 3), turn(y, 2)),
        (x, "x", turn(x, 1), turn(x, 3), turn(x, 2)),
    )
    straight = chunks - DIRECT

    def send(k, f, n, src, inbox, where):
        return remote(src, inbox, ws_sem.at[n], wr_sem.at[k, f, n], where)

    def copies(k, f, stage):
        p, axis, right, left, away = ways[f if stage < 2 else 1 - f]
        right_id, left_id, far_id = {axis: right}, {axis: left}, {axis: away}
        if stage == 0:
            b = dwb.at[k, f, away]
            skip = k // straight
            return [
                send(k, f, 0, b.at[pl.ds(0, 64)], r1.at[k, f, 0], {axis: (p + 1 + skip) % 4}),
                send(k, f, 1, b.at[pl.ds(64, 64)], r1.at[k, f, 1], {axis: (p + 3 - skip) % 4}),
            ]
        if stage == 1:
            return [
                send(k, f, 2, dwb.at[k, f, right], r2.at[k, f, 0], right_id),
                send(k, f, 3, dwb.at[k, f, left], r2.at[k, f, 1], left_id),
            ]
        if stage == 2:
            return [
                send(k, f, 4, e1.at[k, f, away], r3.at[k, f, 2], far_id),
                send(k, f, 5, e1.at[k, f, right], r3.at[k, f, 0], right_id),
                send(k, f, 6, e1.at[k, f, left], r3.at[k, f, 1], left_id),
            ]
        return [send(k, f, 7, f1.at[k, f, 1 - zh], r4.at[k, f], zh_other)]

    def advance(stage, k):
        last = isinstance(k, int) and k >= straight
        for f in range(2):
            for c in copies(k, f, stage - 1):
                c.wait_recv()
            p, _, right, left, _ = ways[f if stage < 3 else 1 - f]
            if stage == 1:
                dwb[k, f, right, :64] = (dwb[k, f, right, :64].astype(F32) + r1[k, f, 0].astype(F32)).astype(BF)
                dwb[k, f, left, 64:] = (dwb[k, f, left, 64:].astype(F32) + r1[k, f, 1].astype(F32)).astype(BF)
            elif stage == 2:
                total = dwb[k, f, p].astype(F32) + r2[k, f, 0].astype(F32) + r2[k, f, 1].astype(F32)
                if last:
                    for c in copies(k, f, 0):
                        c.wait_recv()
                    total += r1[k, f].reshape(128, 256).astype(F32)
                e1[k, f] = total.astype(BF).reshape(4, 32, 256)
            elif stage == 3:
                total = e1[k, f, p].astype(F32)
                for q in range(3):
                    total += r3[k, f, q].astype(F32)
                f1[k, f] = total.astype(BF).reshape(2, 16, 256)
            else:
                dw_o[2 * k + f] = f1[k, f, zh].astype(F32) + r4[k, f].astype(F32)
            if stage < 4:
                for c in copies(k, f, stage):
                    c.start()

    send1 = remote(dcs.at[other], c1, cs_sem.at[0], cr_sem.at[0], core_other)

    def pack_latent():
        for b in range(GROUP):
            for s in range(8):
                r0 = (b * 8 + s) * 24
                dcs[s % 2, (b % 2) * 4 + s // 2, b // 2, :, :latent] = acc[r0 : r0 + 24].astype(BF)
                dcs[s % 2, (b % 2) * 4 + s // 2, b // 2, :, latent:] = racc[r0 : r0 + 24].astype(BF)
        send1.start()

    def chunk_step(t, carry):
        weighed = [weigh(2 * t + f) for f in range(2)]
        for f in range(2):
            grads(2 * t + f, f, *weighed[f])
        both = dot(kvg[0], wcat[2 * t], NT) + dot(kvg[1], wcat[2 * t + 1], NT)
        acc[...] += both
        pl.when(t == chunks - 1)(pack_latent)
        for f in range(2):
            dwb[t, f] = dot(lat_t[f], kvg[f]).astype(BF).reshape(4, 128, 256)
        for f in range(2):
            for c in copies(t, f, 0):
                c.start()

        @pl.when(t >= straight)
        def _():
            for f in range(2):
                for c in copies(t, f, 1):
                    c.start()

        for stage in [q for q in range(1, 5) if LAG[q] < chunks]:
            @pl.when(t >= LAG[stage])
            def _():
                advance(stage, t - LAG[stage])
        return carry

    lax.fori_loop(0, chunks, chunk_step, 0)

    sends2 = [
        remote(s1.at[z_pos[k]], c2.at[k], cs_sem.at[2 + k], cr_sem.at[2 + k], z_ring[k]) for k in range(7)
    ]
    send3 = remote(s2.at[1 - x_lo], c3, cs_sem.at[1], cr_sem.at[1], x_other)

    def tail(t):
        for stage in range(1, 5):
            k = t - LAG[stage]
            if 0 <= k < (straight if stage == 1 else chunks):
                advance(stage, k)

    out_copies = [
        pltpu.make_async_copy(dqn.at[pl.ds(0, rows * heads)], dq_o.at[:, pl.ds(0, 128)], in_sem.at[0]),
        pltpu.make_async_copy(dqr.at[pl.ds(0, rows * heads)], dq_o.at[:, pl.ds(128, 128)], in_sem.at[1]),
    ]
    for c in out_copies:
        c.start()
    send1.wait_recv()
    s1[...] = (dcs[core].astype(F32) + c1[...].astype(F32)).astype(BF)
    for s in sends2:
        s.start()
    for t in range(chunks, chunks + LAG[3]):
        tail(t)
    across = s1[zpos].astype(F32)
    for k, s in enumerate(sends2):
        s.wait_recv()
        across += c2[k].astype(F32)
    s2[...] = across.astype(BF)
    send3.start()
    for t in range(chunks + LAG[3], chunks + LAG[4]):
        tail(t)
    send3.wait_recv()
    dc_o[...] = s2[x_lo].astype(F32) + c3[...].astype(F32)

    for c in out_copies:
        c.wait()
    send1.wait_send()
    send3.wait_send()
    for s in sends2:
        s.wait_send()

    for n, sent in enumerate((r1, r1, r2, r2, r3, r3, r3, r4)):
        whole = sent.at[:, :, 0] if n < 7 else sent
        remote(whole, whole, ws_sem.at[n], wr_sem.at[0, 0, n], core_other).wait_send()


def per_device(compressed, query, d_output, w_uk, w_uv):
    rows, columns = compressed.shape
    latent, heads, nope = w_uk.shape
    width = query.shape[2]
    span = GROUP * rows
    chunks = heads // 2
    anywhere = pl.BlockSpec(memory_space=pl.ANY)
    vmem = pl.BlockSpec(memory_space=pltpu.VMEM)
    dma = pltpu.SemaphoreType.DMA
    dq, dc, dw = pl.pallas_call(
        kernel,
        out_shape=[
            jax.ShapeDtypeStruct((rows * heads, 256), F32),
            jax.ShapeDtypeStruct((24, columns), F32),
            jax.ShapeDtypeStruct((heads, 16, 256), F32),
        ],
        in_specs=[pl.BlockSpec(memory_space=pltpu.HBM)] * 5,
        out_specs=[anywhere, vmem, vmem],
        scratch_shapes=[
            pltpu.VMEM((span, columns), BF),
            pltpu.VMEM((2, latent, heads, 128), BF),
            pltpu.VMEM((rows, heads, width), BF),
            pltpu.VMEM((rows, heads, 128), BF),
            pltpu.VMEM((rows * heads + heads, 128), F32),
            pltpu.VMEM((heads, latent, 256), BF),
            pltpu.VMEM((heads, rows, width), BF),
            pltpu.VMEM((heads, rows, 128), BF),
            pltpu.VMEM((heads, span, 256), BF),
            pltpu.VMEM((2, span, 256), BF),
            pltpu.VMEM((2, latent, span), BF),
            pltpu.VMEM((span, latent), F32),
            pltpu.VMEM((span, width - nope), F32),
            pltpu.VMEM((rows * heads + heads, 128), F32),
            pltpu.VMEM((rows * heads + heads, 128), F32),
            pltpu.VMEM((chunks, 2, 4, 128, 256), BF),
            pltpu.VMEM((chunks, 2, 2, 64, 256), BF),
            pltpu.VMEM((chunks, 2, 2, 128, 256), BF),
            pltpu.VMEM((chunks, 2, 4, 32, 256), BF),
            pltpu.VMEM((chunks, 2, 3, 32, 256), BF),
            pltpu.VMEM((chunks, 2, 2, 16, 256), BF),
            pltpu.VMEM((chunks, 2, 16, 256), BF),
            pltpu.VMEM((2, 8, 2, 24, columns), BF),
            pltpu.VMEM((8, 2, 24, columns), BF),
            pltpu.VMEM((8, 2, 24, columns), BF),
            pltpu.VMEM((7, 2, 24, columns), BF),
            pltpu.VMEM((2, 24, columns), BF),
            pltpu.VMEM((24, columns), BF),
            dma((5,)), dma((7,)), dma((7,)),
            dma((8,)), dma((chunks, 2, 8)), dma((9,)), dma((9,)),
        ],
        compiler_params=pltpu.CompilerParams(
            collective_id=0, has_side_effects=True, vmem_limit_bytes=57 * 2**20
        ),
        cost_estimate=pl.CostEstimate(
            flops=14_000_000_000, bytes_accessed=10_000_000, transcendentals=2_400_000
        ),
    )(compressed, query, d_output, w_uk, w_uv)
    dq = dq.reshape(rows, heads, 256)[:, :, :width]
    dw = jnp.transpose(dw, (1, 0, 2))
    return dq, dc, dw[:, :, :128], dw[:, :, 128:]


def solution(mesh):
    torus = Mesh(mesh.devices.reshape(4, 4, 2, 4, 2), CTX + HEAD)
    return jax.shard_map(
        per_device,
        mesh=torus,
        in_specs=(
            P(CTX, None),
            P(CTX, HEAD, None),
            P(CTX, HEAD, None),
            P(None, HEAD, None),
            P(None, HEAD, None),
        ),
        out_specs=(
            P(CTX, HEAD, None),
            P(CTX + HEAD, None),
            P(CTX, HEAD, None),
            P(CTX, HEAD, None),
        ),
        check_vma=False,
    )
```

```python
import functools
import math

import jax
import jax.numpy as jnp
from jax import lax
from jax.experimental import pallas as pl
from jax.experimental.pallas import tpu as pltpu
from jax.sharding import Mesh
from jax.sharding import PartitionSpec as P

BF = jnp.bfloat16
F32 = jnp.float32
GROUP = 4
LAG = (0, 9, 2, 4, 6)
DIRECT = 8
CTX = ("y", "x", "zh")
HEAD = ("zl", "c")
NN = (((1,), (0,)), ((), ()))
NT = (((1,), (1,)), ((), ()))
TN = (((0,), (0,)), ((), ()))


def dot(a, b, dims=NN):
    return lax.dot_general(a, b, dims, preferred_element_type=F32)


def kernel(
    comp_in, query, d_out, w_uk, w_uv,
    dq_o, dc_o, dw_o,
    comp, wraw, qraw, doraw, tmp, wcat, qh, doh, kv, kvg, lat_t, acc, racc, dqn, dqr,
    dwb, r1, r2, e1, r3, f1, r4,
    dcs, c1, s1, c2, s2, c3,
    in_sem, gs_sem, gr_sem, ws_sem, wr_sem, cs_sem, cr_sem,
):
    heads, rows, width = qh.shape
    span, latent = acc.shape
    half_rows = rows // 2
    scale = 1.0 / math.sqrt(width)
    to_exp2 = scale * math.log2(math.e)
    chunks = heads // 2

    y, x, zh = lax.axis_index("y"), lax.axis_index("x"), lax.axis_index("zh")
    zl, core = lax.axis_index("zl"), lax.axis_index("c")
    other = 1 - core
    x_lo = x % 2
    x_pair = x + 1 - 2 * x_lo
    slab = x_lo * 2 + zh
    zpos = zh * 4 + zl

    def turn(p, k):
        return (p + k) % 4

    x_other, core_other, zh_other = {"x": x_pair}, {"c": other}, {"zh": 1 - zh}
    z_pos = [(zpos + k) % 8 for k in range(1, 8)]
    z_ring = [{"zh": q // 4, "zl": q % 4} for q in z_pos]

    def remote(src, dst, send, recv, where):
        return pltpu.make_async_remote_copy(
            src_ref=src, dst_ref=dst, send_sem=send, recv_sem=recv,
            device_id=where, device_id_type=pl.DeviceIdType.MESH,
        )

    loads = [
        pltpu.make_async_copy(w_uk, wraw.at[0], in_sem.at[0]),
        pltpu.make_async_copy(w_uv, wraw.at[1], in_sem.at[1]),
        pltpu.make_async_copy(query, qraw, in_sem.at[2]),
        pltpu.make_async_copy(d_out, doraw, in_sem.at[3]),
        pltpu.make_async_copy(
            comp_in, comp.at[pl.ds(pl.multiple_of(slab * rows, 64), rows)], in_sem.at[4]
        ),
    ]
    for load in loads:
        load.start()

    barrier = pltpu.get_barrier_semaphore()
    peers = [{axis: turn(p, k)} for axis, p in (("x", x), ("y", y)) for k in (1, 2, 3)] + [core_other] + z_ring
    for peer in peers:
        pl.semaphore_signal(barrier, inc=1, device_id=peer, device_id_type=pl.DeviceIdType.MESH)

    def relayout_weight(t):
        def step(r, carry):
            at = pl.ds(pl.multiple_of(r * 128, 128), 128)
            tmp[pl.ds(0, 128 * heads), :] = wraw[t, at].reshape(128 * heads, 128).astype(F32)
            for h in range(heads):
                wcat[h, at, t * 128 : (t + 1) * 128] = tmp[pl.ds(h, 128, stride=heads), :].astype(BF)
            return carry

        lax.fori_loop(0, latent // 128, step, 0)

    loads[0].wait()
    relayout_weight(0)
    pl.semaphore_wait(barrier, len(peers))

    def part(which, half):
        return comp.at[pl.ds(pl.multiple_of(which * rows + half * half_rows, 32), half_rows)]

    own = comp_in.at[pl.ds(pl.multiple_of(core * half_rows, 32), half_rows)]
    z_slab = x_lo * 2 + 1 - zh
    x_slab = (1 - x_lo) * 2 + zh
    d_slab = (1 - x_lo) * 2 + 1 - zh

    def z_send(k, target):
        return remote(own, part(slab, core), gs_sem.at[k], gr_sem.at[1], {"zh": 1 - zh, "zl": target})

    x_send = remote(own, part(slab, core), gs_sem.at[0], gr_sem.at[0], x_other)
    x_send.start()

    @pl.when(zl == 0)
    def _():
        z_send(1, 3).start()
        z_send(2, 2).start()

    @pl.when(zl == 3)
    def _():
        z_send(1, 0).start()
        z_send(2, 1).start()

    def arrived(which, half, k):
        remote(own, part(which, half), gs_sem.at[0], gr_sem.at[k], core_other).wait_recv()

    def swap(which, k):
        return remote(part(which, core), part(which, core), gs_sem.at[k], gr_sem.at[k], core_other)

    diag_send = remote(part(z_slab, core), part(z_slab, core), gs_sem.at[3], gr_sem.at[2], x_other)
    swaps = [swap(x_slab, 4), swap(z_slab, 5), swap(d_slab, 6)]

    def expand(which):
        at = pl.ds(pl.multiple_of(which * rows, 64), rows)
        piece = comp[at, :latent]

        def step(h, carry):
            kv[2 * h, at] = dot(piece, wcat[2 * h]).astype(BF)
            kv[2 * h + 1, at] = dot(piece, wcat[2 * h + 1]).astype(BF)
            return carry

        lax.fori_loop(0, heads // 2, step, 0)

    loads[1].wait()
    relayout_weight(1)
    arrived(x_slab, core, 0)
    swaps[0].start()
    loads[2].wait()
    loads[3].wait()
    nope = 128
    tmp[: rows * heads] = qraw[:, :, :nope].reshape(rows * heads, nope).astype(F32)
    for h in range(heads):
        qh[h, :, :nope] = tmp[pl.ds(h, rows, stride=heads), :].astype(BF)
    tmp[: rows * heads, : width - nope] = qraw[:, :, nope:].reshape(rows * heads, width - nope).astype(F32)
    for h in range(heads):
        qh[h, :, nope:] = tmp[pl.ds(h, rows, stride=heads), :][:, : width - nope].astype(BF)
    tmp[: rows * heads] = doraw[...].reshape(rows * heads, 128).astype(F32)
    for h in range(heads):
        doh[h] = tmp[pl.ds(h, rows, stride=heads), :].astype(BF)
    arrived(z_slab, core, 1)
    diag_send.start()
    swaps[1].start()
    loads[4].wait()
    expand(slab)
    arrived(x_slab, other, 4)
    expand(x_slab)
    arrived(d_slab, core, 2)
    swaps[2].start()
    arrived(z_slab, other, 5)
    expand(z_slab)
    acc[...] = jnp.zeros_like(acc)
    racc[...] = jnp.zeros_like(racc)
    arrived(d_slab, other, 6)
    expand(d_slab)
    x_send.wait_send()
    diag_send.wait_send()
    for s in swaps:
        s.wait_send()

    @pl.when((zl == 0) | (zl == 3))
    def _():
        z_send(1, 0).wait_send()
        z_send(2, 0).wait_send()

    flipped = comp[:, :latent].T
    lat_t[0] = flipped
    for a in range(4):
        for b in range(4):
            lat_t[1, (b * 4 + a) * 32 : (b * 4 + a + 1) * 32] = flipped[(a * 4 + b) * 32 : (a * 4 + b + 1) * 32]

    def weigh(h):
        keys = jnp.concatenate([kv[h, :, :128], comp[:, latent:]], axis=1)
        qq, dd = qh[h], doh[h]
        scores = dot(qq, keys, NT)
        grad_probs = dot(dd, kv[h, :, 128:], NT)
        top = jnp.max(scores, axis=1, keepdims=True)
        grown = jnp.exp2((scores - top) * to_exp2)
        probs = grown * (1.0 / jnp.sum(grown, axis=1, keepdims=True))
        probs_low = probs.astype(BF)
        delta = jnp.sum(probs_low.astype(F32) * grad_probs, axis=1, keepdims=True)
        score_low = (probs * (grad_probs - delta)).astype(BF)
        return keys, qq, dd, probs_low, score_low

    def grads(h, f, keys, qq, dd, probs_low, score_low):
        d_q = dot(score_low, keys) * scale
        dqn[pl.ds(h, rows, stride=heads), :] = d_q[:, :128]
        dqr[pl.ds(h, rows, stride=heads), :] = jnp.concatenate(
            [d_q[:, 128:], jnp.zeros((rows, 256 - width), F32)], axis=1
        )
        key_grad = dot(score_low, qq, TN) * scale
        kvg[f, :, :128] = key_grad[:, :128].astype(BF)
        racc[...] += key_grad[:, 128:]
        kvg[f, :, 128:] = dot(probs_low, dd, TN).astype(BF)

    ways = (
        (y, "y", turn(y, 1), turn(y, 3), turn(y, 2)),
        (x, "x", turn(x, 1), turn(x, 3), turn(x, 2)),
    )
    straight = chunks - DIRECT

    def send(k, f, n, src, inbox, where):
        return remote(src, inbox, ws_sem.at[n], wr_sem.at[k, f, n], where)

    def copies(k, f, stage):
        p, axis, right, left, away = ways[f if stage < 2 else 1 - f]
        right_id, left_id, far_id = {axis: right}, {axis: left}, {axis: away}
        if stage == 0:
            b = dwb.at[k, f, away]
            skip = 1
            return [
                send(k, f, 0, b.at[pl.ds(0, 64)], r1.at[k, f, 0], {axis: (p + 1 + skip) % 4}),
                send(k, f, 1, b.at[pl.ds(64, 64)], r1.at[k, f, 1], {axis: (p + 3 - skip) % 4}),
            ]
        if stage == 1:
            return [
                send(k, f, 2, dwb.at[k, f, right], r2.at[k, f, 0], right_id),
                send(k, f, 3, dwb.at[k, f, left], r2.at[k, f, 1], left_id),
            ]
        if stage == 2:
            return [
                send(k, f, 4, e1.at[k, f, away], r3.at[k, f, 2], far_id),
                send(k, f, 5, e1.at[k, f, right], r3.at[k, f, 0], right_id),
                send(k, f, 6, e1.at[k, f, left], r3.at[k, f, 1], left_id),
            ]
        return [send(k, f, 7, f1.at[k, f, 1 - zh], r4.at[k, f], zh_other)]

    def advance(stage, k):
        last = True
        for f in range(2):
            for c in copies(k, f, stage - 1):
                c.wait_recv()
            p, _, right, left, _ = ways[f if stage < 3 else 1 - f]
            if stage == 1:
                dwb[k, f, right, :64] = (dwb[k, f, right, :64].astype(F32) + r1[k, f, 0].astype(F32)).astype(BF)
                dwb[k, f, left, 64:] = (dwb[k, f, left, 64:].astype(F32) + r1[k, f, 1].astype(F32)).astype(BF)
            elif stage == 2:
                total = dwb[k, f, p].astype(F32) + r2[k, f, 0].astype(F32) + r2[k, f, 1].astype(F32)
                if last:
                    for c in copies(k, f, 0):
                        c.wait_recv()
                    total += r1[k, f].reshape(128, 256).astype(F32)
                e1[k, f] = total.astype(BF).reshape(4, 32, 256)
            elif stage == 3:
                total = e1[k, f, p].astype(F32)
                for q in range(3):
                    total += r3[k, f, q].astype(F32)
                f1[k, f] = total.astype(BF).reshape(2, 16, 256)
            else:
                dw_o[2 * k + f] = f1[k, f, zh].astype(F32) + r4[k, f].astype(F32)
            if stage < 4:
                for c in copies(k, f, stage):
                    c.start()

    send1 = remote(dcs.at[other], c1, cs_sem.at[0], cr_sem.at[0], core_other)

    def pack_latent():
        for b in range(GROUP):
            for s in range(8):
                r0 = (b * 8 + s) * 24
                dcs[s % 2, (b % 2) * 4 + s // 2, b // 2, :, :latent] = acc[r0 : r0 + 24].astype(BF)
                dcs[s % 2, (b % 2) * 4 + s // 2, b // 2, :, latent:] = racc[r0 : r0 + 24].astype(BF)
        send1.start()

    def chunk_step(t, carry):
        weighed = [weigh(2 * t + f) for f in range(2)]
        for f in range(2):
            grads(2 * t + f, f, *weighed[f])
        both = dot(kvg[0], wcat[2 * t], NT) + dot(kvg[1], wcat[2 * t + 1], NT)
        acc[...] += both
        pl.when(t == chunks - 1)(pack_latent)
        for f in range(2):
            dwb[t, f] = dot(lat_t[f], kvg[f]).astype(BF).reshape(4, 128, 256)
        for f in range(2):
            for c in copies(t, f, 0):
                c.start()

        @pl.when(t >= straight)
        def _():
            for f in range(2):
                for c in copies(t, f, 1):
                    c.start()

        for stage in [q for q in range(1, 5) if LAG[q] < chunks]:
            @pl.when(t >= LAG[stage])
            def _():
                advance(stage, t - LAG[stage])
        return carry

    lax.fori_loop(0, chunks, chunk_step, 0)

    sends2 = [
        remote(s1.at[z_pos[k]], c2.at[k], cs_sem.at[2 + k], cr_sem.at[2 + k], z_ring[k]) for k in range(7)
    ]
    send3 = remote(s2.at[1 - x_lo], c3, cs_sem.at[1], cr_sem.at[1], x_other)

    def tail(t):
        for stage in range(1, 5):
            k = t - LAG[stage]
            if 0 <= k < (straight if stage == 1 else chunks):
                advance(stage, k)

    out_copies = [
        pltpu.make_async_copy(dqn.at[pl.ds(0, rows * heads)], dq_o.at[:, pl.ds(0, 128)], in_sem.at[0]),
        pltpu.make_async_copy(dqr.at[pl.ds(0, rows * heads)], dq_o.at[:, pl.ds(128, 128)], in_sem.at[1]),
    ]
    for c in out_copies:
        c.start()
    send1.wait_recv()
    s1[...] = (dcs[core].astype(F32) + c1[...].astype(F32)).astype(BF)
    for s in sends2:
        s.start()
    for t in range(chunks, chunks + LAG[3]):
        tail(t)
    across = s1[zpos].astype(F32)
    for k, s in enumerate(sends2):
        s.wait_recv()
        across += c2[k].astype(F32)
    s2[...] = across.astype(BF)
    send3.start()
    for t in range(chunks + LAG[3], chunks + LAG[4]):
        tail(t)
    send3.wait_recv()
    dc_o[...] = s2[x_lo].astype(F32) + c3[...].astype(F32)

    for c in out_copies:
        c.wait()
    send1.wait_send()
    send3.wait_send()
    for s in sends2:
        s.wait_send()

    for n, sent in enumerate((r1, r1, r2, r2, r3, r3, r3, r4)):
        whole = sent.at[:, :, 0] if n < 7 else sent
        remote(whole, whole, ws_sem.at[n], wr_sem.at[0, 0, n], core_other).wait_send()


def per_device(compressed, query, d_output, w_uk, w_uv):
    rows, columns = compressed.shape
    latent, heads, nope = w_uk.shape
    width = query.shape[2]
    span = GROUP * rows
    chunks = heads // 2
    anywhere = pl.BlockSpec(memory_space=pl.ANY)
    vmem = pl.BlockSpec(memory_space=pltpu.VMEM)
    dma = pltpu.SemaphoreType.DMA
    dq, dc, dw = pl.pallas_call(
        kernel,
        out_shape=[
            jax.ShapeDtypeStruct((rows * heads, 256), F32),
            jax.ShapeDtypeStruct((24, columns), F32),
            jax.ShapeDtypeStruct((heads, 16, 256), F32),
        ],
        in_specs=[pl.BlockSpec(memory_space=pltpu.HBM)] * 5,
        out_specs=[anywhere, vmem, vmem],
        scratch_shapes=[
            pltpu.VMEM((span, columns), BF),
            pltpu.VMEM((2, latent, heads, 128), BF),
            pltpu.VMEM((rows, heads, width), BF),
            pltpu.VMEM((rows, heads, 128), BF),
            pltpu.VMEM((rows * heads + heads, 128), F32),
            pltpu.VMEM((heads, latent, 256), BF),
            pltpu.VMEM((heads, rows, width), BF),
            pltpu.VMEM((heads, rows, 128), BF),
            pltpu.VMEM((heads, span, 256), BF),
            pltpu.VMEM((2, span, 256), BF),
            pltpu.VMEM((2, latent, span), BF),
            pltpu.VMEM((span, latent), F32),
            pltpu.VMEM((span, width - nope), F32),
            pltpu.VMEM((rows * heads + heads, 128), F32),
            pltpu.VMEM((rows * heads + heads, 128), F32),
            pltpu.VMEM((chunks, 2, 4, 128, 256), BF),
            pltpu.VMEM((chunks, 2, 2, 64, 256), BF),
            pltpu.VMEM((chunks, 2, 2, 128, 256), BF),
            pltpu.VMEM((chunks, 2, 4, 32, 256), BF),
            pltpu.VMEM((chunks, 2, 3, 32, 256), BF),
            pltpu.VMEM((chunks, 2, 2, 16, 256), BF),
            pltpu.VMEM((chunks, 2, 16, 256), BF),
            pltpu.VMEM((2, 8, 2, 24, columns), BF),
            pltpu.VMEM((8, 2, 24, columns), BF),
            pltpu.VMEM((8, 2, 24, columns), BF),
            pltpu.VMEM((7, 2, 24, columns), BF),
            pltpu.VMEM((2, 24, columns), BF),
            pltpu.VMEM((24, columns), BF),
            dma((5,)), dma((7,)), dma((7,)),
            dma((8,)), dma((chunks, 2, 8)), dma((9,)), dma((9,)),
        ],
        compiler_params=pltpu.CompilerParams(
            collective_id=0, has_side_effects=True, vmem_limit_bytes=57 * 2**20
        ),
        cost_estimate=pl.CostEstimate(
            flops=14_000_000_000, bytes_accessed=10_000_000, transcendentals=2_400_000
        ),
    )(compressed, query, d_output, w_uk, w_uv)
    dq = dq.reshape(rows, heads, 256)[:, :, :width]
    dw = jnp.transpose(dw, (1, 0, 2))
    return dq, dc, dw[:, :, :128], dw[:, :, 128:]


def solution(mesh):
    torus = Mesh(mesh.devices.reshape(4, 4, 2, 4, 2), CTX + HEAD)
    return jax.shard_map(
        per_device,
        mesh=torus,
        in_specs=(
            P(CTX, None),
            P(CTX, HEAD, None),
            P(CTX, HEAD, None),
            P(None, HEAD, None),
            P(None, HEAD, None),
        ),
        out_specs=(
            P(CTX, HEAD, None),
            P(CTX + HEAD, None),
            P(CTX, HEAD, None),
            P(CTX, HEAD, None),
        ),
        check_vma=False,
    )
```

```python
import functools
import math

import jax
import jax.numpy as jnp
from jax import lax
from jax.experimental import pallas as pl
from jax.experimental.pallas import tpu as pltpu
from jax.sharding import Mesh
from jax.sharding import PartitionSpec as P

BF = jnp.bfloat16
F32 = jnp.float32
GROUP = 4
LAG = (0, 9, 2, 4, 6)
DIRECT = 8
CTX = ("y", "x", "zh")
HEAD = ("zl", "c")
NN = (((1,), (0,)), ((), ()))
NT = (((1,), (1,)), ((), ()))
TN = (((0,), (0,)), ((), ()))


def dot(a, b, dims=NN):
    return lax.dot_general(a, b, dims, preferred_element_type=F32)


def kernel(
    comp_in, query, d_out, w_uk, w_uv,
    dq_o, dc_o, dw_o,
    comp, wraw, qraw, doraw, tmp, wcat, qh, doh, kv, kvg, lat_t, acc, racc, dqn, dqr,
    dwb, r1, r2, e1, r3, f1, r4,
    dcs, c1, s1, c2, s2, c3,
    in_sem, gs_sem, gr_sem, ws_sem, wr_sem, cs_sem, cr_sem,
):
    heads, rows, width = qh.shape
    span, latent = acc.shape
    half_rows = rows // 2
    scale = 1.0 / math.sqrt(width)
    to_exp2 = scale * math.log2(math.e)
    chunks = heads // 2

    y, x, zh = lax.axis_index("y"), lax.axis_index("x"), lax.axis_index("zh")
    zl, core = lax.axis_index("zl"), lax.axis_index("c")
    other = 1 - core
    x_lo = x % 2
    x_pair = x + 1 - 2 * x_lo
    slab = x_lo * 2 + zh
    zpos = zh * 4 + zl

    def turn(p, k):
        return (p + k) % 4

    x_other, core_other, zh_other = {"x": x_pair}, {"c": other}, {"zh": 1 - zh}
    z_pos = [(zpos + k) % 8 for k in range(1, 8)]
    z_ring = [{"zh": q // 4, "zl": q % 4} for q in z_pos]

    def remote(src, dst, send, recv, where):
        return pltpu.make_async_remote_copy(
            src_ref=src, dst_ref=dst, send_sem=send, recv_sem=recv,
            device_id=where, device_id_type=pl.DeviceIdType.MESH,
        )

    loads = [
        pltpu.make_async_copy(w_uk, wraw.at[0], in_sem.at[0]),
        pltpu.make_async_copy(w_uv, wraw.at[1], in_sem.at[1]),
        pltpu.make_async_copy(query, qraw, in_sem.at[2]),
        pltpu.make_async_copy(d_out, doraw, in_sem.at[3]),
        pltpu.make_async_copy(
            comp_in, comp.at[pl.ds(pl.multiple_of(slab * rows, 64), rows)], in_sem.at[4]
        ),
    ]
    for load in loads:
        load.start()

    barrier = pltpu.get_barrier_semaphore()
    peers = [{axis: turn(p, k)} for axis, p in (("x", x), ("y", y)) for k in (1, 2, 3)] + [core_other] + z_ring
    for peer in peers:
        pl.semaphore_signal(barrier, inc=1, device_id=peer, device_id_type=pl.DeviceIdType.MESH)

    def relayout_weight(t):
        def step(r, carry):
            at = pl.ds(pl.multiple_of(r * 128, 128), 128)
            tmp[pl.ds(0, 128 * heads), :] = wraw[t, at].reshape(128 * heads, 128).astype(F32)
            for h in range(heads):
                wcat[h, at, t * 128 : (t + 1) * 128] = tmp[pl.ds(h, 128, stride=heads), :].astype(BF)
            return carry

        lax.fori_loop(0, latent // 128, step, 0)

    loads[0].wait()
    relayout_weight(0)
    pl.semaphore_wait(barrier, len(peers))

    def part(which, half):
        return comp.at[pl.ds(pl.multiple_of(which * rows + half * half_rows, 32), half_rows)]

    own = comp_in.at[pl.ds(pl.multiple_of(core * half_rows, 32), half_rows)]
    z_slab = x_lo * 2 + 1 - zh
    x_slab = (1 - x_lo) * 2 + zh
    d_slab = (1 - x_lo) * 2 + 1 - zh

    quarter = half_rows // 2

    def own_piece(s):
        return comp_in.at[pl.ds(pl.multiple_of(core * half_rows + s * quarter, 16), quarter)]

    def piece(which, half, s):
        return comp.at[pl.ds(pl.multiple_of(which * rows + half * half_rows + s * quarter, 16), quarter)]

    def z_send(k, s, target):
        where = {"zh": 1 - zh, "zl": target}
        return remote(own_piece(s), piece(slab, core, s), gs_sem.at[1 + 2 * k + s], gr_sem.at[1 + s], where)

    x_send = remote(own, part(slab, core), gs_sem.at[0], gr_sem.at[0], x_other)
    x_send.start()

    @pl.when(zl == 0)
    def _():
        for s in range(2):
            z_send(0, s, 3).start()
            z_send(1, s, 2).start()

    @pl.when(zl == 3)
    def _():
        for s in range(2):
            z_send(0, s, 0).start()
            z_send(1, s, 1).start()

    def arrived(which, half, k):
        remote(own, part(which, half), gs_sem.at[0], gr_sem.at[k], core_other).wait_recv()

    def piece_arrived(which, half, s, k):
        remote(own_piece(0), piece(which, half, s), gs_sem.at[0], gr_sem.at[k], core_other).wait_recv()

    def swap(which, k):
        return remote(part(which, core), part(which, core), gs_sem.at[k], gr_sem.at[k], core_other)

    diag_sends = [
        remote(piece(z_slab, core, s), piece(z_slab, core, s), gs_sem.at[5 + s], gr_sem.at[3 + s], x_other)
        for s in range(2)
    ]
    swaps = [swap(x_slab, 7), swap(z_slab, 8)] + [
        remote(piece(d_slab, core, s), piece(d_slab, core, s), gs_sem.at[9 + s], gr_sem.at[9 + s], core_other)
        for s in range(2)
    ]

    def expand(which, first, last):
        at = pl.ds(pl.multiple_of(which * rows, 64), rows)
        piece_rows = comp[at, :latent]

        def step(h, carry):
            kv[2 * h, at] = dot(piece_rows, wcat[2 * h]).astype(BF)
            kv[2 * h + 1, at] = dot(piece_rows, wcat[2 * h + 1]).astype(BF)
            return carry

        lax.fori_loop(first // 2, last // 2, step, 0)

    loads[1].wait()
    relayout_weight(1)
    arrived(x_slab, core, 0)
    swaps[0].start()
    loads[2].wait()
    loads[3].wait()
    nope = 128
    tmp[: rows * heads] = qraw[:, :, :nope].reshape(rows * heads, nope).astype(F32)
    for h in range(heads):
        qh[h, :, :nope] = tmp[pl.ds(h, rows, stride=heads), :].astype(BF)
    tmp[: rows * heads, : width - nope] = qraw[:, :, nope:].reshape(rows * heads, width - nope).astype(F32)
    for h in range(heads):
        qh[h, :, nope:] = tmp[pl.ds(h, rows, stride=heads), :][:, : width - nope].astype(BF)
    tmp[: rows * heads] = doraw[...].reshape(rows * heads, 128).astype(F32)
    for h in range(heads):
        doh[h] = tmp[pl.ds(h, rows, stride=heads), :].astype(BF)
    piece_arrived(z_slab, core, 0, 1)
    diag_sends[0].start()
    loads[4].wait()
    expand(slab, 0, heads)
    piece_arrived(z_slab, core, 1, 2)
    diag_sends[1].start()
    swaps[1].start()
    arrived(x_slab, other, 7)
    expand(x_slab, 0, heads)
    piece_arrived(d_slab, core, 0, 3)
    swaps[2].start()
    arrived(z_slab, other, 8)
    expand(z_slab, 0, heads // 2)
    piece_arrived(d_slab, core, 1, 4)
    swaps[3].start()
    expand(z_slab, heads // 2, heads)
    acc[...] = jnp.zeros_like(acc)
    racc[...] = jnp.zeros_like(racc)
    piece_arrived(d_slab, other, 0, 9)
    piece_arrived(d_slab, other, 1, 10)
    expand(d_slab, 0, heads)
    x_send.wait_send()
    for s in diag_sends + swaps:
        s.wait_send()

    @pl.when((zl == 0) | (zl == 3))
    def _():
        for s in range(2):
            z_send(0, s, 0).wait_send()
            z_send(1, s, 0).wait_send()

    flipped = comp[:, :latent].T
    lat_t[0] = flipped
    for a in range(4):
        for b in range(4):
            lat_t[1, (b * 4 + a) * 32 : (b * 4 + a + 1) * 32] = flipped[(a * 4 + b) * 32 : (a * 4 + b + 1) * 32]

    def weigh(h):
        keys = jnp.concatenate([kv[h, :, :128], comp[:, latent:]], axis=1)
        qq, dd = qh[h], doh[h]
        scores = dot(qq, keys, NT)
        grad_probs = dot(dd, kv[h, :, 128:], NT)
        top = jnp.max(scores, axis=1, keepdims=True)
        grown = jnp.exp2((scores - top) * to_exp2)
        probs = grown * (1.0 / jnp.sum(grown, axis=1, keepdims=True))
        probs_low = probs.astype(BF)
        delta = jnp.sum(probs_low.astype(F32) * grad_probs, axis=1, keepdims=True)
        score_low = (probs * (grad_probs - delta)).astype(BF)
        return keys, qq, dd, probs_low, score_low

    def grads(h, f, keys, qq, dd, probs_low, score_low):
        d_q = dot(score_low, keys) * scale
        dqn[pl.ds(h, rows, stride=heads), :] = d_q[:, :128]
        dqr[pl.ds(h, rows, stride=heads), :] = jnp.concatenate(
            [d_q[:, 128:], jnp.zeros((rows, 256 - width), F32)], axis=1
        )
        key_grad = dot(score_low, qq, TN) * scale
        kvg[f, :, :128] = key_grad[:, :128].astype(BF)
        racc[...] += key_grad[:, 128:]
        kvg[f, :, 128:] = dot(probs_low, dd, TN).astype(BF)

    ways = (
        (y, "y", turn(y, 1), turn(y, 3), turn(y, 2)),
        (x, "x", turn(x, 1), turn(x, 3), turn(x, 2)),
    )
    straight = chunks - DIRECT

    def send(k, f, n, src, inbox, where):
        return remote(src, inbox, ws_sem.at[n], wr_sem.at[k, f, n], where)

    def copies(k, f, stage):
        p, axis, right, left, away = ways[f if stage < 2 else 1 - f]
        right_id, left_id, far_id = {axis: right}, {axis: left}, {axis: away}
        if stage == 0:
            b = dwb.at[k, f, away]
            skip = 1
            return [
                send(k, f, 0, b.at[pl.ds(0, 64)], r1.at[k, f, 0], {axis: (p + 1 + skip) % 4}),
                send(k, f, 1, b.at[pl.ds(64, 64)], r1.at[k, f, 1], {axis: (p + 3 - skip) % 4}),
            ]
        if stage == 1:
            return [
                send(k, f, 2, dwb.at[k, f, right], r2.at[k, f, 0], right_id),
                send(k, f, 3, dwb.at[k, f, left], r2.at[k, f, 1], left_id),
            ]
        if stage == 2:
            return [
                send(k, f, 4, e1.at[k, f, away], r3.at[k, f, 2], far_id),
                send(k, f, 5, e1.at[k, f, right], r3.at[k, f, 0], right_id),
                send(k, f, 6, e1.at[k, f, left], r3.at[k, f, 1], left_id),
            ]
        return [send(k, f, 7, f1.at[k, f, 1 - zh], r4.at[k, f], zh_other)]

    def advance(stage, k):
        last = True
        for f in range(2):
            for c in copies(k, f, stage - 1):
                c.wait_recv()
            p, _, right, left, _ = ways[f if stage < 3 else 1 - f]
            if stage == 1:
                dwb[k, f, right, :64] = (dwb[k, f, right, :64].astype(F32) + r1[k, f, 0].astype(F32)).astype(BF)
                dwb[k, f, left, 64:] = (dwb[k, f, left, 64:].astype(F32) + r1[k, f, 1].astype(F32)).astype(BF)
            elif stage == 2:
                total = dwb[k, f, p].astype(F32) + r2[k, f, 0].astype(F32) + r2[k, f, 1].astype(F32)
                if last:
                    for c in copies(k, f, 0):
                        c.wait_recv()
                    total += r1[k, f].reshape(128, 256).astype(F32)
                e1[k, f] = total.astype(BF).reshape(4, 32, 256)
            elif stage == 3:
                total = e1[k, f, p].astype(F32)
                for q in range(3):
                    total += r3[k, f, q].astype(F32)
                f1[k, f] = total.astype(BF).reshape(2, 16, 256)
            else:
                dw_o[2 * k + f] = f1[k, f, zh].astype(F32) + r4[k, f].astype(F32)
            if stage < 4:
                for c in copies(k, f, stage):
                    c.start()

    send1 = remote(dcs.at[other], c1, cs_sem.at[0], cr_sem.at[0], core_other)

    def pack_latent():
        for b in range(GROUP):
            for s in range(8):
                r0 = (b * 8 + s) * 24
                dcs[s % 2, (b % 2) * 4 + s // 2, b // 2, :, :latent] = acc[r0 : r0 + 24].astype(BF)
                dcs[s % 2, (b % 2) * 4 + s // 2, b // 2, :, latent:] = racc[r0 : r0 + 24].astype(BF)
        send1.start()

    def chunk_step(t, carry):
        weighed = [weigh(2 * t + f) for f in range(2)]
        for f in range(2):
            grads(2 * t + f, f, *weighed[f])
        both = dot(kvg[0], wcat[2 * t], NT) + dot(kvg[1], wcat[2 * t + 1], NT)
        acc[...] += both
        pl.when(t == chunks - 1)(pack_latent)
        for f in range(2):
            dwb[t, f] = dot(lat_t[f], kvg[f]).astype(BF).reshape(4, 128, 256)
        for f in range(2):
            for c in copies(t, f, 0):
                c.start()

        @pl.when(t >= straight)
        def _():
            for f in range(2):
                for c in copies(t, f, 1):
                    c.start()

        for stage in [q for q in range(1, 5) if LAG[q] < chunks]:
            @pl.when(t >= LAG[stage])
            def _():
                advance(stage, t - LAG[stage])
        return carry

    lax.fori_loop(0, chunks, chunk_step, 0)

    sends2 = [
        remote(s1.at[z_pos[k]], c2.at[k], cs_sem.at[2 + k], cr_sem.at[2 + k], z_ring[k]) for k in range(7)
    ]
    send3 = remote(s2.at[1 - x_lo], c3, cs_sem.at[1], cr_sem.at[1], x_other)

    def tail(t):
        for stage in range(1, 5):
            k = t - LAG[stage]
            if 0 <= k < (straight if stage == 1 else chunks):
                advance(stage, k)

    out_copies = [
        pltpu.make_async_copy(dqn.at[pl.ds(0, rows * heads)], dq_o.at[:, pl.ds(0, 128)], in_sem.at[0]),
        pltpu.make_async_copy(dqr.at[pl.ds(0, rows * heads)], dq_o.at[:, pl.ds(128, 128)], in_sem.at[1]),
    ]
    for c in out_copies:
        c.start()
    send1.wait_recv()
    s1[...] = (dcs[core].astype(F32) + c1[...].astype(F32)).astype(BF)
    for s in sends2:
        s.start()
    for t in range(chunks, chunks + LAG[3]):
        tail(t)
    across = s1[zpos].astype(F32)
    for k, s in enumerate(sends2):
        s.wait_recv()
        across += c2[k].astype(F32)
    s2[...] = across.astype(BF)
    send3.start()
    for t in range(chunks + LAG[3], chunks + LAG[4]):
        tail(t)
    send3.wait_recv()
    dc_o[...] = s2[x_lo].astype(F32) + c3[...].astype(F32)

    for c in out_copies:
        c.wait()
    send1.wait_send()
    send3.wait_send()
    for s in sends2:
        s.wait_send()

    for n, sent in enumerate((r1, r1, r2, r2, r3, r3, r3, r4)):
        whole = sent.at[:, :, 0] if n < 7 else sent
        remote(whole, whole, ws_sem.at[n], wr_sem.at[0, 0, n], core_other).wait_send()


def per_device(compressed, query, d_output, w_uk, w_uv):
    rows, columns = compressed.shape
    latent, heads, nope = w_uk.shape
    width = query.shape[2]
    span = GROUP * rows
    chunks = heads // 2
    anywhere = pl.BlockSpec(memory_space=pl.ANY)
    vmem = pl.BlockSpec(memory_space=pltpu.VMEM)
    dma = pltpu.SemaphoreType.DMA
    dq, dc, dw = pl.pallas_call(
        kernel,
        out_shape=[
            jax.ShapeDtypeStruct((rows * heads, 256), F32),
            jax.ShapeDtypeStruct((24, columns), F32),
            jax.ShapeDtypeStruct((heads, 16, 256), F32),
        ],
        in_specs=[pl.BlockSpec(memory_space=pltpu.HBM)] * 5,
        out_specs=[anywhere, vmem, vmem],
        scratch_shapes=[
            pltpu.VMEM((span, columns), BF),
            pltpu.VMEM((2, latent, heads, 128), BF),
            pltpu.VMEM((rows, heads, width), BF),
            pltpu.VMEM((rows, heads, 128), BF),
            pltpu.VMEM((rows * heads + heads, 128), F32),
            pltpu.VMEM((heads, latent, 256), BF),
            pltpu.VMEM((heads, rows, width), BF),
            pltpu.VMEM((heads, rows, 128), BF),
            pltpu.VMEM((heads, span, 256), BF),
            pltpu.VMEM((2, span, 256), BF),
            pltpu.VMEM((2, latent, span), BF),
            pltpu.VMEM((span, latent), F32),
            pltpu.VMEM((span, width - nope), F32),
            pltpu.VMEM((rows * heads + heads, 128), F32),
            pltpu.VMEM((rows * heads + heads, 128), F32),
            pltpu.VMEM((chunks, 2, 4, 128, 256), BF),
            pltpu.VMEM((chunks, 2, 2, 64, 256), BF),
            pltpu.VMEM((chunks, 2, 2, 128, 256), BF),
            pltpu.VMEM((chunks, 2, 4, 32, 256), BF),
            pltpu.VMEM((chunks, 2, 3, 32, 256), BF),
            pltpu.VMEM((chunks, 2, 2, 16, 256), BF),
            pltpu.VMEM((chunks, 2, 16, 256), BF),
            pltpu.VMEM((2, 8, 2, 24, columns), BF),
            pltpu.VMEM((8, 2, 24, columns), BF),
            pltpu.VMEM((8, 2, 24, columns), BF),
            pltpu.VMEM((7, 2, 24, columns), BF),
            pltpu.VMEM((2, 24, columns), BF),
            pltpu.VMEM((24, columns), BF),
            dma((5,)), dma((11,)), dma((11,)),
            dma((8,)), dma((chunks, 2, 8)), dma((9,)), dma((9,)),
        ],
        compiler_params=pltpu.CompilerParams(
            collective_id=0, has_side_effects=True, vmem_limit_bytes=57 * 2**20
        ),
        cost_estimate=pl.CostEstimate(
            flops=14_000_000_000, bytes_accessed=10_000_000, transcendentals=2_400_000
        ),
    )(compressed, query, d_output, w_uk, w_uv)
    dq = dq.reshape(rows, heads, 256)[:, :, :width]
    dw = jnp.transpose(dw, (1, 0, 2))
    return dq, dc, dw[:, :, :128], dw[:, :, 128:]


def solution(mesh):
    torus = Mesh(mesh.devices.reshape(4, 4, 2, 4, 2), CTX + HEAD)
    return jax.shard_map(
        per_device,
        mesh=torus,
        in_specs=(
            P(CTX, None),
            P(CTX, HEAD, None),
            P(CTX, HEAD, None),
            P(None, HEAD, None),
            P(None, HEAD, None),
        ),
        out_specs=(
            P(CTX, HEAD, None),
            P(CTX + HEAD, None),
            P(CTX, HEAD, None),
            P(CTX, HEAD, None),
        ),
        check_vma=False,
    )
```
